256 devices in a mesh: leaf: 256 (over x, z, y, core).
Axes of the slice: x: 4, y: 4, z: 8, core: 2. Of those that a mesh axis runs over, the one named last changes fastest.
Arguments:
- rhs: bfloat16 [524288, 64], P('leaf'), may hold values from -6 to 6
- leaf_inverse: bfloat16 [524288, 2048], P('leaf')
- bases: bfloat16 [3, 524288, 256], P(None, 'leaf'), may hold values from -0.125 to 0.125
- coupling: bfloat16 [3, 256, 256], replicated
Outputs:
- solved: bfloat16 [524288, 64], P('leaf')
The draws below stay inside these ranges and needn't reach their ends.
All inputs are finite; a program needn't handle non-finite values.
Results may differ from the reference program's by a relative error of at most 0.017.
Values sent between devices are 32-bit elements; how exact they have to be, the bound alone decides.
No kernel may reach another device: no remote copies, remote signals or barrier semaphores. Data moves between devices by JAX's collectives and lax.ppermute only.
A program may use at most 64 MiB of HBM per device.

```python
import jax
import jax.numpy as jnp
from jax import lax

LEAF = 2048
RANK = 256
RHS = 64
LEVELS = 3
POINTS = 524288
N_LEAF = 256


def draw_leaf_inverse(key, part):
    key = jax.random.fold_in(key, 11)
    key_off, key_diag = jax.random.split(key)
    shape = (N_LEAF * LEAF, LEAF)
    rows = jnp.arange(N_LEAF * LEAF, dtype=jnp.int32)[:, None] % LEAF
    cols = jnp.arange(LEAF, dtype=jnp.int32)[None, :]
    ondiag = (rows == cols).astype(jnp.float32)
    off = jax.random.normal(key_off, shape, jnp.float32) * (0.5 / LEAF ** 0.5)
    diag = jax.random.uniform(key_diag, shape, jnp.float32, 0.5, 1.5)
    return (off * (1.0 - ondiag) + diag * ondiag).astype(jnp.bfloat16)


def draw_coupling(key, part):
    key = jax.random.fold_in(key, 12)
    level = jnp.arange(LEVELS, dtype=jnp.float32)[:, None, None]
    half = N_LEAF / 2.0 ** (LEVELS - level)
    scale = 1.0 / jnp.sqrt(RANK * half)
    shape = (LEVELS, RANK, RANK)
    base = jax.random.normal(key, shape, jnp.float32)
    return (base * scale).astype(jnp.bfloat16)


def block_levels(rng, dims, shards, least, high):
    factor_of = 1.0
    for dim, parts in shards:
        heights = jax.random.uniform(jax.random.fold_in(jax.random.fold_in(rng, 6), dim), (parts,), jnp.float32, least / len(shards), high / len(shards))
        factor_of = factor_of * jnp.repeat(jnp.exp(heights), dims[dim] // parts).reshape((-1,) + (1,) * (len(dims) - 1 - dim))
    return factor_of


def noise(own_key, dims, deviation, limit, pieces=(), kind=jnp.bfloat16):
    drawn = deviation * jax.random.normal(own_key, dims, jnp.float32)
    if pieces:
        drawn = drawn * block_levels(own_key, dims, pieces, -0.22, 0.18)
    return jnp.clip(drawn, -limit, limit).astype(kind)


def setup_inputs(seed: int = 0) -> dict:
    streams_of = jax.random.split(jax.random.key(seed), 5)
    return {
        "rhs": noise(streams_of[0], (POINTS, RHS), 1.0, 6.0, ((0, 256),)),
        "leaf_inverse": draw_leaf_inverse(jax.random.fold_in(streams_of[4], 71), 0),
        "bases": noise(streams_of[2], (LEVELS, POINTS, RANK), LEAF ** -0.5, 0.125, ((1, 256),)),
        "coupling": draw_coupling(jax.random.fold_in(streams_of[4], 71), 0),
    }


def leaf_products(mats, vecs, transpose):
    def one(pair):
        if transpose:
            return lax.dot_general(pair[0], pair[1], (((0,), (0,)), ((), ())), preferred_element_type=jnp.float32)
        return jnp.dot(pair[0], pair[1], preferred_element_type=jnp.float32)
    return lax.map(one, (mats, vecs))


def apply_level(state, basis, weight, level):
    devices = N_LEAF
    group = devices // 2 ** (LEVELS - 1 - level)
    half = group // 2
    proj = leaf_products(basis, state.astype(jnp.bfloat16), True)
    child = proj.reshape(devices // half, half, RANK, RHS).sum(axis=1)
    other = child.reshape(devices // group, 2, RANK, RHS)[:, ::-1].reshape(devices // half, RANK, RHS)
    coeff = jnp.einsum("ij,njk->nik", weight.astype(jnp.float32), other, precision=lax.Precision.HIGHEST)
    coeff = jnp.repeat(coeff, half, axis=0).astype(jnp.bfloat16)
    return state - leaf_products(basis, coeff, False)


def reference(rhs, leaf_inverse, bases, coupling):
    devices = N_LEAF
    inv = leaf_inverse.reshape(devices, LEAF, LEAF)
    state = leaf_products(inv, rhs.reshape(devices, LEAF, RHS), False)
    basis_all = bases.reshape(LEVELS, devices, LEAF, RANK)
    for level in range(LEVELS):
        state = apply_level(state, basis_all[level], coupling[level], level)
    for level in reversed(range(LEVELS)):
        state = apply_level(state, basis_all[level], coupling[level].T, level)
    solved = leaf_products(inv, state.astype(jnp.bfloat16), True)
    return solved.reshape(devices * LEAF, RHS).astype(jnp.bfloat16)
```

```python
import jax
import jax.numpy as jnp
from jax import lax
from jax.experimental import pallas as pl
from jax.experimental.pallas import tpu as pltpu
from jax.sharding import PartitionSpec as P

F32, BF16 = jnp.float32, jnp.bfloat16
AXIS = "leaf"
N = 256
CHIPS = 128
SMEM, VMEM = pltpu.SMEM, pltpu.VMEM
BLOCK = 256


def params(mib):
    return pltpu.CompilerParams(vmem_limit_bytes=mib << 20)


def cost(flops, size):
    return pl.CostEstimate(flops=flops, bytes_accessed=size, transcendentals=0)


def whole(count, space=None):
    return [pl.BlockSpec(memory_space=space or VMEM)] * count


def dot(a, b, dims=((1,), (0,))):
    return lax.dot_general(a, b, (dims, ((), ())), preferred_element_type=F32)


def high(a, b, dims=((1,), (0,))):
    return lax.dot_general(a, b, (dims, ((), ())), precision=lax.Precision.HIGHEST, preferred_element_type=F32)


NT, TN = ((1,), (1,)), ((0,), (0,))


def rounded(value):
    return value.astype(BF16).astype(F32)


def swap(value, mask):
    return lax.ppermute(value, AXIS, [(i, i ^ mask) for i in range(N)])


def line(size, stride):
    return [
        [base + low + stride * k for k in range(size)]
        for base in range(0, N, size * stride)
        for low in range(stride)
    ]


def over_chips(value):
    return lax.all_to_all(value, AXIS, 0, 0, axis_index_groups=line(CHIPS, 2), tiled=True)


def pick(index, low, high):
    return jnp.where(index == 0, low, high)


def xor_order(parts, y):
    a, b, c, d = parts
    one = y & 1
    a, b, c, d = pick(one, a, b), pick(one, b, a), pick(one, c, d), pick(one, d, c)
    two = y & 2
    return pick(two, a, c), pick(two, b, d), pick(two, c, a), pick(two, d, b)


def halve(value, core):
    half = value.shape[0] // 2
    low, high_ = value[:half], value[half:]
    return pick(core, low, high_) + swap(pick(core, high_, low), 1)


def unhalve(value, core):
    other = swap(value, 1)
    return jnp.concatenate([pick(core, value, other), pick(core, other, value)], axis=0)


def gram_kernel(core_ref, u_ref, keep_ref, send_ref, acc):
    step = pl.program_id(0)
    rank = u_ref.shape[2]

    @pl.when(step == 0)
    def _():
        acc[...] = jnp.zeros_like(acc)

    for place, (a, b) in enumerate(((1, 0), (1, 1), (1, 2), (2, 0), (2, 2))):
        acc[:, place * rank : (place + 1) * rank] += dot(u_ref[a], u_ref[b], TN)

    @pl.when(step == pl.num_programs(0) - 1)
    def _():
        half = rank // 2
        low = core_ref[0] == 0
        keep_ref[...] = jnp.where(low, acc[:half], acc[half:])
        send_ref[...] = jnp.where(low, acc[half:], acc[:half])


def gram(core, bases):
    levels, leaf, rank = bases.shape
    rows = min(512, leaf)
    shape = jax.ShapeDtypeStruct((rank // 2, 5 * rank), F32)
    return pl.pallas_call(
        gram_kernel,
        grid=(leaf // rows,),
        in_specs=[
            pl.BlockSpec(memory_space=SMEM),
            pl.BlockSpec((levels, rows, rank), lambda i: (0, i, 0)),
        ],
        out_specs=[pl.BlockSpec((rank // 2, 5 * rank), lambda i: (0, 0))] * 2,
        out_shape=[shape, shape],
        scratch_shapes=[pltpu.VMEM((rank, 5 * rank), F32)],
        compiler_params=params(32),
        cost_estimate=cost(10 * leaf * rank * rank, 6 * leaf * rank),
        name="gram",
    )(core, bases)


def table_kernel(rows_ref, out_ref):
    width = rows_ref.shape[2]
    rank = width // 5
    sub = [rows_ref[16 * c : 16 * c + 16].sum(axis=0) for c in range(8)]
    node = [sub[2 * c] + sub[2 * c + 1] for c in range(4)]
    child = [node[0] + node[1], node[2] + node[3]]
    for c in range(8):
        other, beside, across = sub[c ^ 1], node[(c >> 1) ^ 1], child[(c >> 2) ^ 1]
        row = jnp.concatenate(
            [
                other[:, :rank],
                beside[:, rank : 3 * rank],
                other[:, 3 * rank : 4 * rank],
                across[:, 4 * rank :],
            ],
            axis=1,
        )
        out_ref[16 * c : 16 * c + 16] = jnp.broadcast_to(row[None], (16, 1, width))


def table(rows):
    return pl.pallas_call(
        table_kernel,
        in_specs=whole(1),
        out_specs=whole(1)[0],
        out_shape=jax.ShapeDtypeStruct(rows.shape, F32),
        compiler_params=params(32),
        cost_estimate=cost(rows.size, 8 * rows.size),
        name="table",
    )(rows)


def first_kernel(b_ref, f_ref, u_ref, z_ref, p_ref, bt):
    step = pl.program_id(0)

    @pl.when(step == 0)
    def _():
        bt[...] = b_ref[...].astype(F32).T.astype(BF16)
        p_ref[...] = jnp.zeros_like(p_ref)

    z = dot(bt[...], f_ref[...], NT)
    z_ref[...] = z
    p_ref[...] += dot(z.astype(BF16), u_ref[0])


def first(rhs, inverse, bases):
    leaf, cols = rhs.shape
    rank = bases.shape[2]
    return pl.pallas_call(
        first_kernel,
        grid=(leaf // BLOCK,),
        in_specs=[
            pl.BlockSpec((leaf, cols), lambda i: (0, 0)),
            pl.BlockSpec((BLOCK, leaf), lambda i: (i, 0)),
            pl.BlockSpec((1, BLOCK, rank), lambda i: (0, i, 0)),
        ],
        out_specs=[
            pl.BlockSpec((cols, BLOCK), lambda i: (0, i)),
            pl.BlockSpec((cols, rank), lambda i: (0, 0)),
        ],
        out_shape=[
            jax.ShapeDtypeStruct((cols, leaf), F32),
            jax.ShapeDtypeStruct((cols, rank), F32),
        ],
        scratch_shapes=[pltpu.VMEM((cols, leaf), BF16)],
        compiler_params=params(32),
        cost_estimate=cost(2 * leaf * leaf * cols, 2 * leaf * leaf),
        name="first",
    )(rhs, inverse, bases)


def project_kernel(q_ref, u_ref, z_ref, new_ref, s_ref):
    rank = u_ref.shape[2]
    new = z_ref[...] - dot(q_ref[...].astype(BF16), u_ref[0], NT)
    new_ref[...] = new
    zb = new.astype(BF16)
    for level in range(3):
        s_ref[:, level * rank : (level + 1) * rank] = dot(zb, u_ref[level])


def project(q, bases, state):
    cols, leaf = state.shape
    rank = bases.shape[2]
    return pl.pallas_call(
        project_kernel,
        in_specs=whole(3),
        out_specs=whole(2),
        out_shape=[
            jax.ShapeDtypeStruct((cols, leaf), F32),
            jax.ShapeDtypeStruct((cols, 3 * rank), F32),
        ],
        compiler_params=params(32),
        cost_estimate=cost(8 * leaf * rank * cols, 6 * leaf * rank),
        name="project",
    )(q, bases, state)


def last_kernel(q_ref, u_ref, z_ref, f_ref, out_ref, acc):
    step = pl.program_id(0)
    rank = u_ref.shape[2]

    @pl.when(step == 0)
    def _():
        acc[...] = jnp.zeros_like(acc)

    z = z_ref[...]
    for level in range(3):
        z -= dot(q_ref[:, level * rank : (level + 1) * rank].astype(BF16), u_ref[level], NT)
    acc[...] += dot(z.astype(BF16), f_ref[...])

    @pl.when(step == pl.num_programs(0) - 1)
    def _():
        out_ref[...] = acc[...].T.astype(BF16)


def last(q, bases, state, inverse):
    cols, leaf = state.shape
    rank = bases.shape[2]
    return pl.pallas_call(
        last_kernel,
        grid=(leaf // BLOCK,),
        in_specs=[
            pl.BlockSpec((cols, 3 * rank), lambda i: (0, 0)),
            pl.BlockSpec((3, BLOCK, rank), lambda i: (0, i, 0)),
            pl.BlockSpec((cols, BLOCK), lambda i: (0, i)),
            pl.BlockSpec((BLOCK, leaf), lambda i: (i, 0)),
        ],
        out_specs=pl.BlockSpec((leaf, cols), lambda i: (0, 0)),
        out_shape=jax.ShapeDtypeStruct((leaf, cols), BF16),
        scratch_shapes=[pltpu.VMEM((cols, leaf), F32)],
        compiler_params=params(32),
        cost_estimate=cost(2 * leaf * leaf * cols, 2 * leaf * leaf),
        name="last",
    )(q, bases, state, inverse)


def shards(rhs, leaf_inverse, bases, coupling):
    index = lax.axis_index(AXIS)
    core, y = index & 1, (index >> 1) & 3
    rank, cols = bases.shape[2], rhs.shape[1]
    w0, w1, w2 = (coupling[k].astype(F32) for k in range(3))

    keep, send = gram(core.reshape(1), bases)
    mine = (keep + swap(send, 1)).reshape(CHIPS, 1, 5 * rank)
    mine, rhs = lax.optimization_barrier((mine, rhs))
    back = over_chips(table(over_chips(mine))).reshape(CHIPS, 5 * rank)
    sums = unhalve(back, core)
    m10, m11, m12, m20, m22 = (sums[:, k * rank : (k + 1) * rank] for k in range(5))

    state, proj = first(rhs, leaf_inverse, bases)

    half = halve(proj, core)
    half = half + swap(half, 2) + swap(half, 4) + swap(half, 6)
    pair = half + swap(half, 8)
    other = swap(pair, 40) + swap(pair, 56)
    q0 = unhalve(high(other, w0, NT), core)

    state, proj = project(q0, bases, state)
    half = halve(proj, core)
    eighth = cols // 8
    parts = xor_order([half[k * eighth : (k + 1) * eighth] for k in range(4)], y)
    part = parts[0] + swap(parts[1], 2) + swap(parts[2], 4) + swap(parts[3], 6)
    pair = part + swap(part, 8)
    own = pair[:, rank:] + swap(pair[:, rank:], 16)
    other = swap(pair, 40) + swap(pair, 56)
    s0o, node = other[:, :rank], own + other[:, rank:]
    s1, s2 = node[:, :rank], node[:, rank:]

    q1o = high(s1, w1, NT)
    v = s2 - high(rounded(q1o), m12)
    beside = swap(jnp.concatenate([v, s1], axis=1), 64)
    c2, s1o = v + beside[:, :rank], beside[:, rank:]
    c2o = swap(v, 128) + swap(v, 192)
    q1 = high(s1o, w1, NT)
    q2 = high(c2o, w2, NT)
    q2o = high(c2, w2, NT)
    t2 = q2 + high(c2o - high(rounded(q2o), m22), w2)
    t1 = q1 + high(s1o - high(rounded(q1o), m11) - high(rounded(t2), m12, NT), w1)
    t0 = high(s0o - high(rounded(t1), m10) - high(rounded(t2), m20), w0)

    mine = jnp.concatenate([t0, t1, t2], axis=1)
    parts = [mine, swap(mine, 2), swap(mine, 4), swap(mine, 6)]
    half = jnp.concatenate(xor_order(parts, y), axis=0)
    return last(unhalve(half, core), bases, state, leaf_inverse)


def solution(mesh):
    placed = (P(AXIS, None), P(AXIS, None), P(None, AXIS, None), P())
    return jax.shard_map(
        shards, mesh=mesh, in_specs=placed, out_specs=P(AXIS, None), check_vma=False
    )
```

```python
import jax
import jax.numpy as jnp
from jax import lax
from jax.experimental import pallas as pl
from jax.experimental.pallas import tpu as pltpu
from jax.sharding import PartitionSpec as P

F32, BF16 = jnp.float32, jnp.bfloat16
AXIS = "leaf"
N = 256
VMEM = pltpu.VMEM
CHUNKS = 4


def params(mib):
    return pltpu.CompilerParams(vmem_limit_bytes=mib << 20)


def cost(flops, size):
    return pl.CostEstimate(flops=flops, bytes_accessed=size, transcendentals=0)


def whole(count, space=None):
    return [pl.BlockSpec(memory_space=space or VMEM)] * count


def dot(a, b, dims=((1,), (0,))):
    return lax.dot_general(a, b, (dims, ((), ())), preferred_element_type=F32)


NN, NT, TN = ((1,), (0,)), ((1,), (1,)), ((0,), (0,))


def swap(value, mask):
    return lax.ppermute(value, AXIS, [(i, i ^ mask) for i in range(N)])


def line(size, stride):
    return [
        [base + low + stride * k for k in range(size)]
        for base in range(0, N, size * stride)
        for low in range(stride)
    ]


def over_chips(value):
    groups = [[(xz * 4 + y) * 2 + core for y in range(4) for xz in range(32)] for core in range(2)]
    return lax.all_to_all(value, AXIS, 0, 0, axis_index_groups=groups, tiled=True)


def over_xz(value):
    return lax.all_to_all(value, AXIS, 0, 0, axis_index_groups=line(32, 8), tiled=True)


def thrice(value):
    a = value.astype(BF16)
    rest = value - a.astype(F32)
    b = rest.astype(BF16)
    return jnp.concatenate([a, b, (rest - b.astype(F32)).astype(BF16)], axis=0)


def exact(value, weight, dims):
    rows = value.shape[0]
    out = dot(thrice(value), weight, dims)
    return out[:rows] + out[rows : 2 * rows] + out[2 * rows :]


def apply(value, matrix, dims):
    value, top = value.astype(BF16), matrix.astype(BF16)
    return dot(value, top, dims) + dot(value, (matrix - top.astype(F32)).astype(BF16), dims)


def core_index():
    return lax.axis_index(AXIS) & 1


def both(own, other):
    low = core_index() == 0
    return jnp.concatenate([jnp.where(low, own, other), jnp.where(low, other, own)], axis=0)


def split_halves(value, keep_ref, send_ref):
    half = value.shape[0] // 2
    low = core_index() == 0
    keep_ref[...] = jnp.where(low, value[:half], value[half:])
    send_ref[...] = jnp.where(low, value[half:], value[:half])


def split_kernel(keep_ref, other_ref, *outs):
    rows = outs[0].shape[0]
    y = (lax.axis_index(AXIS) >> 1) & 3
    for m, out in enumerate(outs):
        at = pl.ds(pl.multiple_of((y ^ m) * rows, rows), rows)
        out[...] = keep_ref[at, :] + other_ref[at, :]


def split(keep, other):
    shape = jax.ShapeDtypeStruct((keep.shape[0] // 4, keep.shape[1]), F32)
    return pl.pallas_call(
        split_kernel,
        in_specs=whole(2),
        out_specs=whole(4),
        out_shape=[shape] * 4,
        compiler_params=params(16),
        cost_estimate=cost(keep.size, 12 * keep.size),
        name="split",
    )(keep, other)


def join_kernel(*refs):
    parts, out_ref = refs[:4], refs[4]
    rows = parts[0].shape[0]
    y = (lax.axis_index(AXIS) >> 1) & 3
    for m, part in enumerate(parts):
        at = pl.ds(pl.multiple_of((y ^ m) * rows, rows), rows)
        out_ref[at, :] = part[...].reshape(rows, out_ref.shape[1])


def join(parts):
    rows, width = parts[0].shape[0], parts[0].shape[-1]
    return pl.pallas_call(
        join_kernel,
        in_specs=whole(4),
        out_specs=whole(1)[0],
        out_shape=jax.ShapeDtypeStruct((4 * rows, width), F32),
        compiler_params=params(16),
        cost_estimate=cost(0, 32 * rows * width),
        name="join",
    )(*parts)


def add_kernel(a, b, out):
    out[...] = (a[...] + b[...]).reshape(out.shape)


def add_rows(a, b):
    rows, width = a.shape
    return pl.pallas_call(
        add_kernel,
        in_specs=whole(2),
        out_specs=whole(1)[0],
        out_shape=jax.ShapeDtypeStruct((rows, 1, width), F32),
        compiler_params=params(16),
        cost_estimate=cost(rows * width, 12 * rows * width),
        name="add_rows",
    )(a, b)


def table_kernel(rows_ref, out_ref):
    rank = rows_ref.shape[2] // 6
    sub = []
    for c in range(8):
        total = rows_ref[4 * c : 4 * c + 4].sum(axis=0)
        for y in range(1, 4):
            total += rows_ref[32 * y + 4 * c : 32 * y + 4 * c + 4].sum(axis=0)
        sub.append(total)
    node = [sub[2 * c] + sub[2 * c + 1] for c in range(4)]
    child = [node[0] + node[1], node[2] + node[3]]
    for c in range(8):
        own, other, beside, across = sub[c], sub[c ^ 1], node[(c >> 1) ^ 1], child[(c >> 2) ^ 1]
        row = jnp.concatenate(
            [own[:, : 2 * rank], other[:, : 3 * rank], beside[:, 3 * rank : 5 * rank], across[:, 5 * rank :]], axis=1
        )
        out_ref[4 * c : 4 * c + 4] = jnp.broadcast_to(row[None], (4, 1, row.shape[1]))


def table(rows):
    return pl.pallas_call(
        table_kernel,
        in_specs=whole(1),
        out_specs=whole(1)[0],
        out_shape=jax.ShapeDtypeStruct((32, 1, rows.shape[2] // 6 * 8), F32),
        compiler_params=params(16),
        cost_estimate=cost(rows.size, 8 * rows.size),
        name="table",
    )(rows)


PAIRS = ((1, 0), (2, 0), (0, 0), (1, 1), (1, 2), (2, 2))


def gram_kernel(u_ref, keep_ref, send_ref, u_buf, g_buf, sems):
    rank = u_ref.shape[2]
    copies = [pltpu.make_async_copy(u_ref.at[k], u_buf.at[k], sems.at[k]) for k in range(3)]
    for copy in copies:
        copy.start()
    ready = 0
    for a, b in sorted(PAIRS, key=max):
        while ready <= max(a, b):
            copies[ready].wait()
            ready += 1
        place = PAIRS.index((a, b))
        g_buf[:, place * rank : (place + 1) * rank] = dot(u_buf[a], u_buf[b], TN)
    split_halves(g_buf[...], keep_ref, send_ref)


def gram(bases):
    levels, leaf, rank = bases.shape
    width = len(PAIRS) * rank
    shape = jax.ShapeDtypeStruct((rank // 2, width), F32)
    return pl.pallas_call(
        gram_kernel,
        in_specs=whole(1, pl.ANY),
        out_specs=whole(2),
        out_shape=[shape, shape],
        scratch_shapes=[
            pltpu.VMEM((levels, leaf, rank), BF16),
            pltpu.VMEM((rank, width), F32),
            pltpu.SemaphoreType.DMA((levels,)),
        ],
        compiler_params=params(56),
        cost_estimate=cost(12 * leaf * rank * rank, 6 * leaf * rank),
        name="gram",
    )(bases)


def first_kernel(b_ref, f_ref, u_ref, z_ref, keep_ref, send_ref, f_buf, u_buf, sems):
    leaf = f_ref.shape[0]
    rows = leaf // CHUNKS
    copies = [
        pltpu.make_async_copy(f_ref.at[pl.ds(i * rows, rows)], f_buf.at[pl.ds(i * rows, rows)], sems.at[i])
        for i in range(CHUNKS)
    ]
    copies.append(pltpu.make_async_copy(u_ref, u_buf, sems.at[CHUNKS]))
    for copy in copies:
        copy.start()
    b = b_ref[...]
    for i in range(CHUNKS):
        copies[i].wait()
        z_ref[:, i * rows : (i + 1) * rows] = dot(b, f_buf[i * rows : (i + 1) * rows], NT)
    copies[CHUNKS].wait()
    zb = z_ref[...].astype(BF16)
    split_halves(jnp.concatenate([dot(zb, u_buf[k]) for k in range(3)], axis=1), keep_ref, send_ref)


def first(rhs, inverse, bases):
    cols, leaf = rhs.shape
    rank = bases.shape[2]
    shape = jax.ShapeDtypeStruct((cols // 2, 3 * rank), F32)
    return pl.pallas_call(
        first_kernel,
        in_specs=whole(1) + whole(2, pl.ANY),
        out_specs=whole(3),
        out_shape=[jax.ShapeDtypeStruct((cols, leaf), F32), shape, shape],
        scratch_shapes=[
            pltpu.VMEM((leaf, leaf), BF16),
            pltpu.VMEM((3, leaf, rank), BF16),
            pltpu.SemaphoreType.DMA((CHUNKS + 1,)),
        ],
        compiler_params=params(56),
        cost_estimate=cost(2 * leaf * leaf * cols, 2 * leaf * leaf),
        name="first",
    )(rhs, inverse, bases)


def block(own_ref, other_ref, place):
    rank = own_ref.shape[1] // 8
    at = slice(place * rank, (place + 1) * rank)
    return both(own_ref[:, at], other_ref[:, at])


def up_kernel(own_ref, other_ref, w_ref, p_ref, po_ref, vs_ref, q_ref):
    m10, m20, m10o, m20o, m00o, _, m12o = (block(own_ref, other_ref, k) for k in range(7))
    rank = m10.shape[0]
    q0 = exact(po_ref[:, :rank], w_ref[0], NT)
    q0o = exact(p_ref[:, :rank], w_ref[0], NT)
    s0o = po_ref[:, :rank] - apply(q0o, m00o, NN)
    s1 = p_ref[:, rank : 2 * rank] + po_ref[:, rank : 2 * rank] - apply(q0, m10, NT) - apply(q0o, m10o, NT)
    s2 = p_ref[:, 2 * rank :] + po_ref[:, 2 * rank :] - apply(q0, m20, NT) - apply(q0o, m20o, NT)
    q1o = exact(s1, w_ref[1], NT)
    vs_ref[...] = jnp.concatenate([s2 - apply(q1o, m12o, NN), s1], axis=1)
    q_ref[...] = jnp.concatenate([s0o, q0, q1o], axis=1)


def up(own, other, coupling, p, po):
    rows, width = p.shape
    rank = width // 3
    return pl.pallas_call(
        up_kernel,
        in_specs=whole(5),
        out_specs=whole(2),
        out_shape=[jax.ShapeDtypeStruct((rows, 2 * rank), F32), jax.ShapeDtypeStruct((rows, width), F32)],
        compiler_params=params(16),
        cost_estimate=cost(32 * rows * rank * rank, 8 * own.size),
        name="up",
    )(own, other, coupling, p, po)


def down_kernel(own_ref, other_ref, w_ref, vs_ref, b_ref, r2_ref, r3_ref, q_ref, out_ref):
    m10o, m20o, _, m11o, m12o, m22o = (block(own_ref, other_ref, k) for k in range(2, 8))
    rank = m10o.shape[0]
    s0o, q0, q1o = (q_ref[:, k * rank : (k + 1) * rank] for k in range(3))
    c2 = vs_ref[:, :rank] + b_ref[:, :rank]
    c2o = r2_ref[...] + r3_ref[...]
    s1o = b_ref[:, rank:]
    q1 = exact(s1o, w_ref[1], NT)
    q2 = exact(c2o, w_ref[2], NT)
    q2o = exact(c2, w_ref[2], NT)
    t2 = q2 + exact(c2o - apply(q2o, m22o, NN), w_ref[2], NN)
    t1 = q1 + exact(s1o - apply(q1o, m11o, NN) - apply(t2, m12o, NT), w_ref[1], NN)
    t0 = q0 + exact(s0o - apply(t1, m10o, NN) - apply(t2, m20o, NN), w_ref[0], NN)
    out_ref[...] = jnp.concatenate([t0, t1, t2], axis=1)


def down(own, other, coupling, vs, beside, r2, r3, q):
    rows, width = q.shape
    return pl.pallas_call(
        down_kernel,
        in_specs=whole(8),
        out_specs=whole(1)[0],
        out_shape=jax.ShapeDtypeStruct((rows, width), F32),
        compiler_params=params(16),
        cost_estimate=cost(4 * rows * width * width, 8 * own.size),
        name="down",
    )(own, other, coupling, vs, beside, r2, r3, q)


def last_kernel(own_ref, other_ref, u_ref, z_ref, f_ref, out_ref):
    leaf = f_ref.shape[0]
    rank = u_ref.shape[2]
    width = leaf // CHUNKS
    q = both(own_ref[...], other_ref[...]).astype(BF16)
    z = z_ref[...]
    for level in range(3):
        z -= dot(q[:, level * rank : (level + 1) * rank], u_ref[level], NT)
    zb = z.astype(BF16)
    for i in range(CHUNKS):
        at = slice(i * width, (i + 1) * width)
        out_ref[:, at] = dot(zb, f_ref[:, at]).astype(BF16)


def last(own, other, bases, state, inverse):
    cols, leaf = state.shape
    return pl.pallas_call(
        last_kernel,
        in_specs=whole(5),
        out_specs=whole(1)[0],
        out_shape=jax.ShapeDtypeStruct((cols, leaf), BF16),
        compiler_params=params(24),
        cost_estimate=cost(2 * leaf * leaf * cols, 2 * leaf * leaf),
        name="last",
    )(own, other, bases, state, inverse)


def after(value, *others):
    return lax.optimization_barrier((value, *others))[0]


def shards(rhs, leaf_inverse, bases, coupling):
    rank = bases.shape[2]

    keep, send = gram(bases)
    mine = add_rows(keep, swap(send, 1))
    summed = table(over_chips(mine))

    state, keep, send = first(after(rhs.T, mine), leaf_inverse, bases)
    parts = split(keep, swap(send, 1))
    part = parts[0] + swap(parts[1], 2) + swap(parts[2], 4) + swap(parts[3], 6)
    pair = part + swap(part, 8)
    p = pair + swap(pair, 16)
    po = swap(pair, 40) + swap(pair, 56)

    back = over_xz(after(summed, pair))
    own = join([back] + [swap(back, 2 * m) for m in (1, 2, 3)])
    sums = (own, swap(own, 1), coupling)

    vs, q = up(*sums, p, po)
    v = vs[:, :rank]
    mine = down(*sums, vs, swap(vs, 64), swap(v, 128), swap(v, 192), q)

    half = join([mine, swap(mine, 2), swap(mine, 4), swap(mine, 6)])
    return last(half, swap(half, 1), bases, state, leaf_inverse).T


def solution(mesh):
    placed = (P(AXIS, None), P(AXIS, None), P(None, AXIS, None), P())
    return jax.shard_map(
        shards, mesh=mesh, in_specs=placed, out_specs=P(AXIS, None), check_vma=False
    )
```

```python
import jax
import jax.numpy as jnp
from jax import lax
from jax.experimental import pallas as pl
from jax.experimental.pallas import tpu as pltpu
from jax.sharding import PartitionSpec as P

F32, BF16 = jnp.float32, jnp.bfloat16
AXIS = "leaf"
N = 256
VMEM = pltpu.VMEM
CHUNKS = 4


def params(mib):
    return pltpu.CompilerParams(vmem_limit_bytes=mib << 20)


def cost(flops, size):
    return pl.CostEstimate(flops=flops, bytes_accessed=size, transcendentals=0)


def whole(count, space=None):
    return [pl.BlockSpec(memory_space=space or VMEM)] * count


def dot(a, b, dims=((1,), (0,))):
    return lax.dot_general(a, b, (dims, ((), ())), preferred_element_type=F32)


NN, NT, TN = ((1,), (0,)), ((1,), (1,)), ((0,), (0,))


def swap(value, mask):
    return lax.ppermute(value, AXIS, [(i, i ^ mask) for i in range(N)])


def line(size, stride):
    return [
        [base + low + stride * k for k in range(size)]
        for base in range(0, N, size * stride)
        for low in range(stride)
    ]


def over_xz(value):
    return lax.all_to_all(value, AXIS, 0, 0, axis_index_groups=line(32, 8), tiled=True)


def thrice(value):
    a = value.astype(BF16)
    rest = value - a.astype(F32)
    b = rest.astype(BF16)
    return jnp.concatenate([a, b, (rest - b.astype(F32)).astype(BF16)], axis=0)


def exact(value, weight, dims):
    rows = value.shape[0]
    out = dot(thrice(value), weight, dims)
    return out[:rows] + out[rows : 2 * rows] + out[2 * rows :]


def apply(value, matrix, dims):
    value, top = value.astype(BF16), matrix.astype(BF16)
    return dot(value, top, dims) + dot(value, (matrix - top.astype(F32)).astype(BF16), dims)


def core_index():
    return lax.axis_index(AXIS) & 1


def both(own, other):
    low = core_index() == 0
    return jnp.concatenate([jnp.where(low, own, other), jnp.where(low, other, own)], axis=0)


def split_halves(value, keep_ref, send_ref):
    half = value.shape[0] // 2
    low = core_index() == 0
    keep_ref[...] = jnp.where(low, value[:half], value[half:])
    send_ref[...] = jnp.where(low, value[half:], value[:half])


def split_kernel(keep_ref, other_ref, *outs):
    rows = outs[0].shape[0]
    y = (lax.axis_index(AXIS) >> 1) & 3
    for m, out in enumerate(outs):
        at = pl.ds(pl.multiple_of((y ^ m) * rows, rows), rows)
        out[...] = keep_ref[at, :] + other_ref[at, :]


def split(keep, other):
    shape = jax.ShapeDtypeStruct((keep.shape[0] // 4, keep.shape[1]), F32)
    return pl.pallas_call(
        split_kernel,
        in_specs=whole(2),
        out_specs=whole(4),
        out_shape=[shape] * 4,
        compiler_params=params(16),
        cost_estimate=cost(keep.size, 12 * keep.size),
        name="split",
    )(keep, other)


def join_kernel(*refs):
    parts, out_ref = refs[:4], refs[4]
    rows = parts[0].shape[0]
    y = (lax.axis_index(AXIS) >> 1) & 3
    for m, part in enumerate(parts):
        at = pl.ds(pl.multiple_of((y ^ m) * rows, rows), rows)
        out_ref[at, :] = part[...].reshape(rows, out_ref.shape[1])


def join(parts):
    rows, width = parts[0].shape[0], parts[0].shape[-1]
    return pl.pallas_call(
        join_kernel,
        in_specs=whole(4),
        out_specs=whole(1)[0],
        out_shape=jax.ShapeDtypeStruct((4 * rows, width), F32),
        compiler_params=params(16),
        cost_estimate=cost(0, 32 * rows * width),
        name="join",
    )(*parts)


def add_kernel(a, b, c, d, out):
    out[...] = (a[...] + b[...] + c[...] + d[...]).reshape(out.shape)


def add_rows(parts):
    rows, width = parts[0].shape
    return pl.pallas_call(
        add_kernel,
        in_specs=whole(4),
        out_specs=whole(1)[0],
        out_shape=jax.ShapeDtypeStruct((rows, 1, width), F32),
        compiler_params=params(16),
        cost_estimate=cost(rows * width, 12 * rows * width),
        name="add_rows",
    )(*parts)


def table_kernel(rows_ref, out_ref):
    rank = rows_ref.shape[2] // 6
    sub = [rows_ref[4 * c : 4 * c + 4].sum(axis=0) for c in range(8)]
    node = [sub[2 * c] + sub[2 * c + 1] for c in range(4)]
    child = [node[0] + node[1], node[2] + node[3]]
    for c in range(8):
        own, other, beside, across = sub[c], sub[c ^ 1], node[(c >> 1) ^ 1], child[(c >> 2) ^ 1]
        row = jnp.concatenate(
            [own[:, : 2 * rank], other[:, : 3 * rank], beside[:, 3 * rank : 5 * rank], across[:, 5 * rank :]], axis=1
        )
        out_ref[4 * c : 4 * c + 4] = jnp.broadcast_to(row[None], (4, 1, row.shape[1]))


def table(rows):
    return pl.pallas_call(
        table_kernel,
        in_specs=whole(1),
        out_specs=whole(1)[0],
        out_shape=jax.ShapeDtypeStruct((32, 1, rows.shape[2] // 6 * 8), F32),
        compiler_params=params(16),
        cost_estimate=cost(rows.size, 8 * rows.size),
        name="table",
    )(rows)


PAIRS = ((1, 0), (2, 0), (0, 0), (1, 1), (1, 2), (2, 2))


def gram_kernel(u_ref, keep_ref, send_ref, u_buf, g_buf, sems):
    rank = u_ref.shape[2]
    copies = [pltpu.make_async_copy(u_ref.at[k], u_buf.at[k], sems.at[k]) for k in range(3)]
    for copy in copies:
        copy.start()
    ready = 0
    for a, b in sorted(PAIRS, key=max):
        while ready <= max(a, b):
            copies[ready].wait()
            ready += 1
        place = PAIRS.index((a, b))
        g_buf[:, place * rank : (place + 1) * rank] = dot(u_buf[a], u_buf[b], TN)
    split_halves(g_buf[...], keep_ref, send_ref)


def gram(bases):
    levels, leaf, rank = bases.shape
    width = len(PAIRS) * rank
    shape = jax.ShapeDtypeStruct((rank // 2, width), F32)
    return pl.pallas_call(
        gram_kernel,
        in_specs=whole(1, pltpu.HBM),
        out_specs=whole(2),
        out_shape=[shape, shape],
        scratch_shapes=[
            pltpu.VMEM((levels, leaf, rank), BF16),
            pltpu.VMEM((rank, width), F32),
            pltpu.SemaphoreType.DMA((levels,)),
        ],
        compiler_params=params(56),
        cost_estimate=cost(12 * leaf * rank * rank, 6 * leaf * rank),
        name="gram",
    )(bases)


def first_kernel(b_ref, f_ref, u_ref, z_ref, keep_ref, send_ref, f_buf, u_buf, sems):
    leaf = f_ref.shape[0]
    rows = leaf // CHUNKS
    copies = [
        pltpu.make_async_copy(f_ref.at[pl.ds(i * rows, rows)], f_buf.at[pl.ds(i * rows, rows)], sems.at[i])
        for i in range(CHUNKS)
    ]
    copies.append(pltpu.make_async_copy(u_ref, u_buf, sems.at[CHUNKS]))
    for copy in copies:
        copy.start()
    b = b_ref[...]
    for i in range(CHUNKS):
        copies[i].wait()
        z_ref[:, i * rows : (i + 1) * rows] = dot(b, f_buf[i * rows : (i + 1) * rows], NT)
    copies[CHUNKS].wait()
    zb = z_ref[...].astype(BF16)
    split_halves(jnp.concatenate([dot(zb, u_buf[k]) for k in range(3)], axis=1), keep_ref, send_ref)


def first(rhs, inverse, bases):
    cols, leaf = rhs.shape
    rank = bases.shape[2]
    shape = jax.ShapeDtypeStruct((cols // 2, 3 * rank), F32)
    return pl.pallas_call(
        first_kernel,
        in_specs=whole(1) + whole(2, pltpu.HBM),
        out_specs=whole(3),
        out_shape=[jax.ShapeDtypeStruct((cols, leaf), F32), shape, shape],
        scratch_shapes=[
            pltpu.VMEM((leaf, leaf), BF16),
            pltpu.VMEM((3, leaf, rank), BF16),
            pltpu.SemaphoreType.DMA((CHUNKS + 1,)),
        ],
        compiler_params=params(61),
        cost_estimate=cost(2 * leaf * leaf * cols, 2 * leaf * leaf),
        name="first",
    )(rhs, inverse, bases)


def block(own_ref, other_ref, place):
    rank = own_ref.shape[1] // 8
    at = slice(place * rank, (place + 1) * rank)
    return both(own_ref[:, at], other_ref[:, at])


def up_kernel(own_ref, other_ref, w_ref, both_ref, vs_ref, q_ref):
    m10, m20, m10o, m20o, m00o, _, m12o = (block(own_ref, other_ref, k) for k in range(7))
    rank = m10.shape[0]
    p_ref, po_ref = both_ref[:, : 3 * rank], both_ref[:, 3 * rank :]
    q0 = exact(po_ref[:, :rank], w_ref[0], NT)
    q0o = exact(p_ref[:, :rank], w_ref[0], NT)
    s0o = po_ref[:, :rank] - apply(q0o, m00o, NN)
    s1 = p_ref[:, rank : 2 * rank] + po_ref[:, rank : 2 * rank] - apply(q0, m10, NT) - apply(q0o, m10o, NT)
    s2 = p_ref[:, 2 * rank :] + po_ref[:, 2 * rank :] - apply(q0, m20, NT) - apply(q0o, m20o, NT)
    q1o = exact(s1, w_ref[1], NT)
    vs_ref[...] = jnp.concatenate([s2 - apply(q1o, m12o, NN), s1], axis=1)
    q_ref[...] = jnp.concatenate([s0o, q0, q1o], axis=1)


def up(own, other, coupling, sums):
    rows, width = sums.shape[0], sums.shape[1] // 2
    rank = width // 3
    return pl.pallas_call(
        up_kernel,
        in_specs=whole(4),
        out_specs=whole(2),
        out_shape=[jax.ShapeDtypeStruct((rows, 2 * rank), F32), jax.ShapeDtypeStruct((rows, width), F32)],
        compiler_params=params(16),
        cost_estimate=cost(32 * rows * rank * rank, 8 * own.size),
        name="up",
    )(own, other, coupling, sums)


def down_kernel(own_ref, other_ref, w_ref, vs_ref, b_ref, r2_ref, r3_ref, q_ref, out_ref):
    m10o, m20o, _, m11o, m12o, m22o = (block(own_ref, other_ref, k) for k in range(2, 8))
    rank = m10o.shape[0]
    s0o, q0, q1o = (q_ref[:, k * rank : (k + 1) * rank] for k in range(3))
    c2 = vs_ref[:, :rank] + b_ref[:, :rank]
    c2o = r2_ref[...] + r3_ref[...]
    s1o = b_ref[:, rank:]
    q1 = exact(s1o, w_ref[1], NT)
    q2 = exact(c2o, w_ref[2], NT)
    q2o = exact(c2, w_ref[2], NT)
    t2 = q2 + exact(c2o - apply(q2o, m22o, NN), w_ref[2], NN)
    t1 = q1 + exact(s1o - apply(q1o, m11o, NN) - apply(t2, m12o, NT), w_ref[1], NN)
    t0 = q0 + exact(s0o - apply(t1, m10o, NN) - apply(t2, m20o, NN), w_ref[0], NN)
    out_ref[...] = jnp.concatenate([t0, t1, t2], axis=1)


def down(own, other, coupling, vs, beside, r2, r3, q):
    rows, width = q.shape
    return pl.pallas_call(
        down_kernel,
        in_specs=whole(8),
        out_specs=whole(1)[0],
        out_shape=jax.ShapeDtypeStruct((rows, width), F32),
        compiler_params=params(16),
        cost_estimate=cost(4 * rows * width * width, 8 * own.size),
        name="down",
    )(own, other, coupling, vs, beside, r2, r3, q)


def last_kernel(own_ref, other_ref, u_ref, z_ref, f_ref, out_ref):
    leaf = f_ref.shape[0]
    rank = u_ref.shape[2]
    width = leaf // CHUNKS
    q = both(own_ref[...], other_ref[...]).astype(BF16)
    z = z_ref[...]
    for level in range(3):
        z -= dot(q[:, level * rank : (level + 1) * rank], u_ref[level], NT)
    zb = z.astype(BF16)
    for i in range(CHUNKS):
        at = slice(i * width, (i + 1) * width)
        out_ref[:, at] = dot(zb, f_ref[:, at]).astype(BF16)


def last(own, other, bases, state, inverse):
    cols, leaf = state.shape
    return pl.pallas_call(
        last_kernel,
        in_specs=whole(5),
        out_specs=whole(1)[0],
        out_shape=jax.ShapeDtypeStruct((cols, leaf), BF16),
        compiler_params=params(24),
        cost_estimate=cost(2 * leaf * leaf * cols, 2 * leaf * leaf),
        name="last",
    )(own, other, bases, state, inverse)


def stage_kernel(f_ref, u_ref, f_out, u_out, sems):
    rows = f_ref.shape[0] // 8
    copies = [
        pltpu.make_async_copy(f_ref.at[pl.ds(i * rows, rows)], f_out.at[pl.ds(i * rows, rows)], sems.at[i])
        for i in range(8)
    ]
    copies.append(pltpu.make_async_copy(u_ref, u_out, sems.at[8]))
    for copy in copies:
        copy.start()
    for copy in copies:
        copy.wait()


def stage(inverse, bases):
    return pl.pallas_call(
        stage_kernel,
        in_specs=whole(2, pltpu.HBM),
        out_specs=whole(2),
        out_shape=[pltpu.VMEM(inverse.shape, BF16), pltpu.VMEM(bases.shape, BF16)],
        scratch_shapes=[pltpu.SemaphoreType.DMA((9,))],
        compiler_params=params(48),
        cost_estimate=cost(0, 4 * inverse.size),
        name="stage",
    )(inverse, bases)


def after(value, *others):
    return lax.optimization_barrier((value, *others))[0]


def shards(rhs, leaf_inverse, bases, coupling):
    rank = bases.shape[2]

    keep, send = gram(bases)
    rows = split(keep, swap(send, 1))
    state, keep, send = first(after(rhs.T, *rows), leaf_inverse, bases)
    parts = split(keep, swap(send, 1))
    mine = add_rows([rows[0]] + [swap(rows[m], 2 * m) for m in (1, 2, 3)])
    summed = table(over_xz(after(mine, parts[0])))
    part = parts[0] + swap(parts[1], 2) + swap(parts[2], 4) + swap(parts[3], 6)
    pair = part + swap(part, 8)
    back = over_xz(after(summed, pair))
    p = pair + swap(pair, 16)
    po = swap(pair, 40) + swap(pair, 56)

    back, mine = lax.optimization_barrier((back, jnp.concatenate([p, po], axis=1)))
    parts = [swap(back, 2 * m) for m in (1, 2, 3)]
    half = join([mine] + [swap(mine, 2 * m) for m in (1, 2, 3)])
    own = join([after(back, half)] + parts)
    sums = (own, swap(own, 1), coupling)

    vs, q = up(*sums, half)
    v = vs[:, :rank]
    inverse_v, bases_v = stage(*lax.optimization_barrier((leaf_inverse, bases, q))[:2])
    mine = down(*sums, vs, swap(vs, 64), swap(v, 128), swap(v, 192), after(q, inverse_v))
    return last(mine, swap(mine, 1), bases_v, state, inverse_v).T


def solution(mesh):
    placed = (P(AXIS, None), P(AXIS, None), P(None, AXIS, None), P())
    return jax.shard_map(
        shards, mesh=mesh, in_specs=placed, out_specs=P(AXIS, None), check_vma=False
    )
```

```python
import jax
import jax.numpy as jnp
from jax import lax
from jax.experimental import pallas as pl
from jax.experimental.pallas import tpu as pltpu
from jax.sharding import PartitionSpec as P

F32, BF16 = jnp.float32, jnp.bfloat16
AXIS = "leaf"
N = 256
VMEM = pltpu.VMEM
CHUNKS = 4


def params(mib):
    return pltpu.CompilerParams(vmem_limit_bytes=mib << 20)


def cost(flops, size):
    return pl.CostEstimate(flops=flops, bytes_accessed=size, transcendentals=0)


def whole(count, space=None):
    return [pl.BlockSpec(memory_space=space or VMEM)] * count


def dot(a, b, dims=((1,), (0,))):
    return lax.dot_general(a, b, (dims, ((), ())), preferred_element_type=F32)


NN, NT, TN = ((1,), (0,)), ((1,), (1,)), ((0,), (0,))


def swap(value, mask):
    return lax.ppermute(value, AXIS, [(i, i ^ mask) for i in range(N)])


def line(size, stride):
    return [
        [base + low + stride * k for k in range(size)]
        for base in range(0, N, size * stride)
        for low in range(stride)
    ]


def over_xz(value):
    return lax.all_to_all(value, AXIS, 0, 0, axis_index_groups=line(32, 8), tiled=True)


def thrice(value):
    a = value.astype(BF16)
    rest = value - a.astype(F32)
    b = rest.astype(BF16)
    return jnp.concatenate([a, b, (rest - b.astype(F32)).astype(BF16)], axis=0)


def exact(value, weight, dims):
    rows = value.shape[0]
    out = dot(thrice(value), weight, dims)
    return out[:rows] + out[rows : 2 * rows] + out[2 * rows :]


def apply(value, matrix, dims):
    value, top = value.astype(BF16), matrix.astype(BF16)
    return dot(value, top, dims) + dot(value, (matrix - top.astype(F32)).astype(BF16), dims)


def core_index():
    return lax.axis_index(AXIS) & 1


def both(own, other):
    low = core_index() == 0
    return jnp.concatenate([jnp.where(low, own, other), jnp.where(low, other, own)], axis=0)


def split_halves(value, keep_ref, send_ref):
    half = value.shape[0] // 2
    low = core_index() == 0
    keep_ref[...] = jnp.where(low, value[:half], value[half:])
    send_ref[...] = jnp.where(low, value[half:], value[:half])


def split_kernel(keep_ref, other_ref, *outs):
    rows = outs[0].shape[0]
    y = (lax.axis_index(AXIS) >> 1) & 3
    for m, out in enumerate(outs):
        at = pl.ds(pl.multiple_of((y ^ m) * rows, rows), rows)
        out[...] = keep_ref[at, :] + other_ref[at, :]


def split(keep, other):
    shape = jax.ShapeDtypeStruct((keep.shape[0] // 4, keep.shape[1]), F32)
    return pl.pallas_call(
        split_kernel,
        in_specs=whole(2),
        out_specs=whole(4),
        out_shape=[shape] * 4,
        compiler_params=params(16),
        cost_estimate=cost(keep.size, 12 * keep.size),
        name="split",
    )(keep, other)


def pack_kernel(sums_ref, p_ref, po_ref, out_ref):
    rows, rank = sums_ref.shape[0], p_ref.shape[1] // 3
    out_ref[:rows] = sums_ref[...]
    for k in range(6):
        value = (p_ref if k < 3 else po_ref)[:, k % 3 * rank : (k % 3 + 1) * rank]
        for r in range(value.shape[0]):
            out_ref[rows + k, :, r * rank : (r + 1) * rank] = value[r : r + 1]


def pack(sums, p, po):
    rows, _, width = sums.shape
    return pl.pallas_call(
        pack_kernel,
        in_specs=whole(3),
        out_specs=whole(1)[0],
        out_shape=jax.ShapeDtypeStruct((rows + 6, 1, width), F32),
        compiler_params=params(16),
        cost_estimate=cost(0, 8 * rows * width),
        name="pack",
    )(sums, p, po)


def unpack_kernel(*refs):
    parts, own_ref, half_ref = refs[:4], refs[4], refs[5]
    rows, rank = own_ref.shape[0] // 4, half_ref.shape[1] // 6
    cols = half_ref.shape[0] // 4
    y = (lax.axis_index(AXIS) >> 1) & 3
    for m, part in enumerate(parts):
        at = pl.ds(pl.multiple_of((y ^ m) * rows, rows), rows)
        own_ref[at, :] = part[:rows].reshape(rows, own_ref.shape[1])
        at = pl.ds(pl.multiple_of((y ^ m) * cols, cols), cols)
        for k in range(6):
            row = part[rows + k]
            value = jnp.concatenate([row[:, r * rank : (r + 1) * rank] for r in range(cols)], axis=0)
            half_ref[at, k * rank : (k + 1) * rank] = value


def unpack(parts, cols, rank):
    rows, width = parts[0].shape[0] - 6, parts[0].shape[2]
    return pl.pallas_call(
        unpack_kernel,
        in_specs=whole(4),
        out_specs=whole(2),
        out_shape=[jax.ShapeDtypeStruct((4 * rows, width), F32), jax.ShapeDtypeStruct((4 * cols, 6 * rank), F32)],
        compiler_params=params(16),
        cost_estimate=cost(0, 32 * rows * width),
        name="unpack",
    )(*parts)


def add_kernel(a, b, c, d, out):
    out[...] = (a[...] + b[...] + c[...] + d[...]).reshape(out.shape)


def add_rows(parts):
    rows, width = parts[0].shape
    return pl.pallas_call(
        add_kernel,
        in_specs=whole(4),
        out_specs=whole(1)[0],
        out_shape=jax.ShapeDtypeStruct((rows, 1, width), F32),
        compiler_params=params(16),
        cost_estimate=cost(rows * width, 12 * rows * width),
        name="add_rows",
    )(*parts)


def table_kernel(rows_ref, out_ref):
    rank = rows_ref.shape[2] // 6
    sub = [rows_ref[4 * c : 4 * c + 4].sum(axis=0) for c in range(8)]
    node = [sub[2 * c] + sub[2 * c + 1] for c in range(4)]
    child = [node[0] + node[1], node[2] + node[3]]
    for c in range(8):
        own, other, beside, across = sub[c], sub[c ^ 1], node[(c >> 1) ^ 1], child[(c >> 2) ^ 1]
        row = jnp.concatenate(
            [own[:, : 2 * rank], other[:, : 3 * rank], beside[:, 3 * rank : 5 * rank], across[:, 5 * rank :]], axis=1
        )
        out_ref[4 * c : 4 * c + 4] = jnp.broadcast_to(row[None], (4, 1, row.shape[1]))


def table(rows):
    return pl.pallas_call(
        table_kernel,
        in_specs=whole(1),
        out_specs=whole(1)[0],
        out_shape=jax.ShapeDtypeStruct((32, 1, rows.shape[2] // 6 * 8), F32),
        compiler_params=params(16),
        cost_estimate=cost(rows.size, 8 * rows.size),
        name="table",
    )(rows)


PAIRS = ((1, 0), (2, 0), (0, 0), (1, 1), (1, 2), (2, 2))


def gram_kernel(u_ref, keep_ref, send_ref, g_buf):
    rank = u_ref.shape[2]
    for place, (a, b) in enumerate(PAIRS):
        g_buf[:, place * rank : (place + 1) * rank] = dot(u_ref[a], u_ref[b], TN)
    split_halves(g_buf[...], keep_ref, send_ref)


def gram(bases):
    leaf, rank = bases.shape[1:]
    width = len(PAIRS) * rank
    shape = jax.ShapeDtypeStruct((rank // 2, width), F32)
    return pl.pallas_call(
        gram_kernel,
        in_specs=whole(1),
        out_specs=whole(2),
        out_shape=[shape, shape],
        scratch_shapes=[pltpu.VMEM((rank, width), F32)],
        compiler_params=params(24),
        cost_estimate=cost(12 * leaf * rank * rank, 6 * leaf * rank),
        name="gram",
    )(bases)


def first_kernel(b_ref, f_ref, u_ref, z_ref, keep_ref, send_ref, f_buf, u_buf, sems):
    leaf = f_ref.shape[0]
    rows = leaf // CHUNKS
    copies = [
        pltpu.make_async_copy(f_ref.at[pl.ds(i * rows, rows)], f_buf.at[pl.ds(i * rows, rows)], sems.at[i])
        for i in range(CHUNKS)
    ]
    copies.append(pltpu.make_async_copy(u_ref, u_buf, sems.at[CHUNKS]))
    for copy in copies:
        copy.start()
    b = b_ref[...]
    for i in range(CHUNKS):
        copies[i].wait()
        z_ref[:, i * rows : (i + 1) * rows] = dot(b, f_buf[i * rows : (i + 1) * rows], NT)
    copies[CHUNKS].wait()
    zb = z_ref[...].astype(BF16)
    split_halves(jnp.concatenate([dot(zb, u_buf[k]) for k in range(3)], axis=1), keep_ref, send_ref)


def first(rhs, inverse, bases):
    cols, leaf = rhs.shape
    rank = bases.shape[2]
    shape = jax.ShapeDtypeStruct((cols // 2, 3 * rank), F32)
    return pl.pallas_call(
        first_kernel,
        in_specs=whole(1) + whole(2, pltpu.HBM),
        out_specs=whole(3),
        out_shape=[jax.ShapeDtypeStruct((cols, leaf), F32), shape, shape],
        scratch_shapes=[
            pltpu.VMEM((leaf, leaf), BF16),
            pltpu.VMEM((3, leaf, rank), BF16),
            pltpu.SemaphoreType.DMA((CHUNKS + 1,)),
        ],
        compiler_params=params(61),
        cost_estimate=cost(2 * leaf * leaf * cols, 2 * leaf * leaf),
        name="first",
    )(rhs, inverse, bases)


def block(own_ref, other_ref, place):
    rank = own_ref.shape[1] // 8
    at = slice(place * rank, (place + 1) * rank)
    return both(own_ref[:, at], other_ref[:, at])


def up_kernel(own_ref, other_ref, w_ref, both_ref, vs_ref, q_ref):
    m10, m20, m10o, m20o, m00o, _, m12o = (block(own_ref, other_ref, k) for k in range(7))
    rank = m10.shape[0]
    p_ref, po_ref = both_ref[:, : 3 * rank], both_ref[:, 3 * rank :]
    q0 = exact(po_ref[:, :rank], w_ref[0], NT)
    q0o = exact(p_ref[:, :rank], w_ref[0], NT)
    s0o = po_ref[:, :rank] - apply(q0o, m00o, NN)
    s1 = p_ref[:, rank : 2 * rank] + po_ref[:, rank : 2 * rank] - apply(q0, m10, NT) - apply(q0o, m10o, NT)
    s2 = p_ref[:, 2 * rank :] + po_ref[:, 2 * rank :] - apply(q0, m20, NT) - apply(q0o, m20o, NT)
    q1o = exact(s1, w_ref[1], NT)
    vs_ref[...] = jnp.concatenate([s2 - apply(q1o, m12o, NN), s1], axis=1)
    q_ref[...] = jnp.concatenate([s0o, q0, q1o], axis=1)


def up(own, other, coupling, sums):
    rows, width = sums.shape[0], sums.shape[1] // 2
    rank = width // 3
    return pl.pallas_call(
        up_kernel,
        in_specs=whole(4),
        out_specs=whole(2),
        out_shape=[jax.ShapeDtypeStruct((rows, 2 * rank), F32), jax.ShapeDtypeStruct((rows, width), F32)],
        compiler_params=params(16),
        cost_estimate=cost(32 * rows * rank * rank, 8 * own.size),
        name="up",
    )(own, other, coupling, sums)


def down_kernel(own_ref, other_ref, w_ref, vs_ref, b_ref, r2_ref, r3_ref, q_ref, out_ref):
    m10o, m20o, _, m11o, m12o, m22o = (block(own_ref, other_ref, k) for k in range(2, 8))
    rank = m10o.shape[0]
    s0o, q0, q1o = (q_ref[:, k * rank : (k + 1) * rank] for k in range(3))
    c2 = vs_ref[:, :rank] + b_ref[:, :rank]
    c2o = r2_ref[...] + r3_ref[...]
    s1o = b_ref[:, rank:]
    q1 = exact(s1o, w_ref[1], NT)
    q2 = exact(c2o, w_ref[2], NT)
    q2o = exact(c2, w_ref[2], NT)
    t2 = q2 + exact(c2o - apply(q2o, m22o, NN), w_ref[2], NN)
    t1 = q1 + exact(s1o - apply(q1o, m11o, NN) - apply(t2, m12o, NT), w_ref[1], NN)
    t0 = q0 + exact(s0o - apply(t1, m10o, NN) - apply(t2, m20o, NN), w_ref[0], NN)
    out_ref[...] = jnp.concatenate([t0, t1, t2], axis=1)


def down(own, other, coupling, vs, beside, r2, r3, q):
    rows, width = q.shape
    return pl.pallas_call(
        down_kernel,
        in_specs=whole(8),
        out_specs=whole(1)[0],
        out_shape=jax.ShapeDtypeStruct((rows, width), F32),
        compiler_params=params(16),
        cost_estimate=cost(4 * rows * width * width, 8 * own.size),
        name="down",
    )(own, other, coupling, vs, beside, r2, r3, q)


def last_kernel(own_ref, other_ref, u_ref, z_ref, f_ref, out_ref):
    leaf = f_ref.shape[0]
    rank = u_ref.shape[2]
    width = leaf // CHUNKS
    q = both(own_ref[...], other_ref[...]).astype(BF16)
    z = z_ref[...]
    for level in range(3):
        z -= dot(q[:, level * rank : (level + 1) * rank], u_ref[level], NT)
    zb = z.astype(BF16)
    for i in range(CHUNKS):
        at = slice(i * width, (i + 1) * width)
        out_ref[:, at] = dot(zb, f_ref[:, at]).astype(BF16)


def last(own, other, bases, state, inverse):
    cols, leaf = state.shape
    return pl.pallas_call(
        last_kernel,
        in_specs=whole(5),
        out_specs=whole(1)[0],
        out_shape=jax.ShapeDtypeStruct((cols, leaf), BF16),
        compiler_params=params(24),
        cost_estimate=cost(2 * leaf * leaf * cols, 2 * leaf * leaf),
        name="last",
    )(own, other, bases, state, inverse)


def stage_kernel(f_ref, u_ref, f_out, u_out, sems):
    rows = f_ref.shape[0] // 8
    copies = [
        pltpu.make_async_copy(f_ref.at[pl.ds(i * rows, rows)], f_out.at[pl.ds(i * rows, rows)], sems.at[i])
        for i in range(8)
    ]
    copies.append(pltpu.make_async_copy(u_ref, u_out, sems.at[8]))
    for copy in copies:
        copy.start()
    for copy in copies:
        copy.wait()


def stage(inverse, bases):
    return pl.pallas_call(
        stage_kernel,
        in_specs=whole(2, pltpu.HBM),
        out_specs=whole(2),
        out_shape=[pltpu.VMEM(inverse.shape, BF16), pltpu.VMEM(bases.shape, BF16)],
        scratch_shapes=[pltpu.SemaphoreType.DMA((9,))],
        compiler_params=params(48),
        cost_estimate=cost(0, 4 * inverse.size),
        name="stage",
    )(inverse, bases)


def after(value, *others):
    return lax.optimization_barrier((value, *others))[0]


def shards(rhs, leaf_inverse, bases, coupling):
    rank = bases.shape[2]

    keep, send = gram(bases)
    rows = split(keep, swap(send, 1))
    state, keep, send = first(after(rhs.T, *rows), leaf_inverse, bases)
    parts = split(keep, swap(send, 1))
    mine = add_rows([rows[0]] + [swap(rows[m], 2 * m) for m in (1, 2, 3)])
    summed = table(over_xz(after(mine, parts[0])))
    part = parts[0] + swap(parts[1], 2) + swap(parts[2], 4) + swap(parts[3], 6)
    pair = part + swap(part, 8)
    back = over_xz(after(summed, pair))
    p = pair + swap(pair, 16)
    po = swap(pair, 40) + swap(pair, 56)

    mine = pack(back, p, po)
    own, half = unpack([mine] + [swap(mine, 2 * m) for m in (1, 2, 3)], p.shape[0], rank)
    sums = (own, swap(own, 1), coupling)

    vs, q = up(*sums, half)
    v = vs[:, :rank]
    inverse_v, bases_v = stage(*lax.optimization_barrier((leaf_inverse, bases, q))[:2])
    mine = down(*sums, vs, swap(vs, 64), swap(v, 128), swap(v, 192), after(q, inverse_v))
    return last(mine, swap(mine, 1), bases_v, state, inverse_v).T


def solution(mesh):
    placed = (P(AXIS, None), P(AXIS, None), P(None, AXIS, None), P())
    return jax.shard_map(
        shards, mesh=mesh, in_specs=placed, out_specs=P(AXIS, None), check_vma=False
    )
```

```python
import jax
import jax.numpy as jnp
from jax import lax
from jax.experimental import pallas as pl
from jax.experimental.pallas import tpu as pltpu
from jax.sharding import PartitionSpec as P

F32, BF16 = jnp.float32, jnp.bfloat16
AXIS = "leaf"
N = 256
VMEM = pltpu.VMEM
CHUNKS = 4


def params(mib):
    return pltpu.CompilerParams(vmem_limit_bytes=mib << 20)


def cost(flops, size):
    return pl.CostEstimate(flops=flops, bytes_accessed=size, transcendentals=0)


def whole(count, space=None):
    return [pl.BlockSpec(memory_space=space or VMEM)] * count


def dot(a, b, dims=((1,), (0,))):
    return lax.dot_general(a, b, (dims, ((), ())), preferred_element_type=F32)


NN, NT, TN = ((1,), (0,)), ((1,), (1,)), ((0,), (0,))


def swap(value, mask):
    return lax.ppermute(value, AXIS, [(i, i ^ mask) for i in range(N)])


def line(size, stride):
    return [
        [base + low + stride * k for k in range(size)]
        for base in range(0, N, size * stride)
        for low in range(stride)
    ]


def over_xz(value):
    return lax.all_to_all(value, AXIS, 0, 0, axis_index_groups=line(32, 8), tiled=True)


def thrice(value):
    a = value.astype(BF16)
    rest = value - a.astype(F32)
    b = rest.astype(BF16)
    return jnp.concatenate([a, b, (rest - b.astype(F32)).astype(BF16)], axis=0)


def exact(value, weight, dims):
    rows = value.shape[0]
    out = dot(thrice(value), weight, dims)
    return out[:rows] + out[rows : 2 * rows] + out[2 * rows :]


def apply(value, matrix, dims):
    value, top = value.astype(BF16), matrix.astype(BF16)
    return dot(value, top, dims) + dot(value, (matrix - top.astype(F32)).astype(BF16), dims)


def core_index():
    return lax.axis_index(AXIS) & 1


def both(own, other):
    low = core_index() == 0
    return jnp.concatenate([jnp.where(low, own, other), jnp.where(low, other, own)], axis=0)


def split_halves(value, keep_ref, send_ref):
    half = value.shape[0] // 2
    low = core_index() == 0
    keep_ref[...] = jnp.where(low, value[:half], value[half:])
    send_ref[...] = jnp.where(low, value[half:], value[:half])


def split_kernel(keep_ref, other_ref, *outs):
    rows = outs[0].shape[0]
    y = (lax.axis_index(AXIS) >> 1) & 3
    for m, out in enumerate(outs):
        at = pl.ds(pl.multiple_of((y ^ m) * rows, rows), rows)
        out[...] = keep_ref[at, :] + other_ref[at, :]


def split(keep, other):
    shape = jax.ShapeDtypeStruct((keep.shape[0] // 4, keep.shape[1]), F32)
    return pl.pallas_call(
        split_kernel,
        in_specs=whole(2),
        out_specs=whole(4),
        out_shape=[shape] * 4,
        compiler_params=params(16),
        cost_estimate=cost(keep.size, 12 * keep.size),
        name="split",
    )(keep, other)


def pack_kernel(sums_ref, p_ref, po_ref, out_ref):
    rows, rank = sums_ref.shape[0], p_ref.shape[1] // 3
    out_ref[:rows] = sums_ref[...]
    for k in range(6):
        value = (p_ref if k < 3 else po_ref)[:, k % 3 * rank : (k % 3 + 1) * rank]
        for r in range(8):
            row, place = divmod(8 * k + r, 7)
            out_ref[rows + row, :, place * rank : (place + 1) * rank] = value[r : r + 1]


def pack(sums, p, po):
    rows, _, width = sums.shape
    return pl.pallas_call(
        pack_kernel,
        in_specs=whole(3),
        out_specs=whole(1)[0],
        out_shape=jax.ShapeDtypeStruct((rows + 7, 1, width), F32),
        compiler_params=params(16),
        cost_estimate=cost(0, 8 * rows * width),
        name="pack",
    )(sums, p, po)


def unpack_kernel(*refs):
    parts, own_ref, half_ref = refs[:4], refs[4], refs[5]
    rows, rank = own_ref.shape[0] // 4, half_ref.shape[1] // 6
    cols = half_ref.shape[0] // 4
    y = (lax.axis_index(AXIS) >> 1) & 3
    for m, part in enumerate(parts):
        at = pl.ds(pl.multiple_of((y ^ m) * rows, rows), rows)
        own_ref[at, :] = part[:rows].reshape(rows, own_ref.shape[1])
        at = pl.ds(pl.multiple_of((y ^ m) * cols, cols), cols)
        for k in range(6):
            places = [divmod(8 * k + r, 7) for r in range(8)]
            value = jnp.concatenate([part[rows + i, :, j * rank : (j + 1) * rank] for i, j in places], axis=0)
            half_ref[at, k * rank : (k + 1) * rank] = value


def unpack(parts, cols, rank):
    rows, width = parts[0].shape[0] - 7, parts[0].shape[2]
    return pl.pallas_call(
        unpack_kernel,
        in_specs=whole(4),
        out_specs=whole(2),
        out_shape=[jax.ShapeDtypeStruct((4 * rows, width), F32), jax.ShapeDtypeStruct((4 * cols, 6 * rank), F32)],
        compiler_params=params(16),
        cost_estimate=cost(0, 32 * rows * width),
        name="unpack",
    )(*parts)


def add_kernel(a, b, c, d, out):
    out[...] = (a[...] + b[...] + c[...] + d[...]).reshape(out.shape)


def add_rows(parts):
    rows, width = parts[0].shape
    return pl.pallas_call(
        add_kernel,
        in_specs=whole(4),
        out_specs=whole(1)[0],
        out_shape=jax.ShapeDtypeStruct((rows, 1, width), F32),
        compiler_params=params(16),
        cost_estimate=cost(rows * width, 12 * rows * width),
        name="add_rows",
    )(*parts)


def table_kernel(rows_ref, out_ref):
    unit = rows_ref.shape[2] // 11
    low = core_index() == 0
    sub = [rows_ref[4 * c : 4 * c + 4].sum(axis=0) for c in range(8)]
    node = [sub[2 * c] + sub[2 * c + 1] for c in range(4)]
    child = [node[0] + node[1], node[2] + node[3]]
    for c in range(8):
        own, other, beside, across = sub[c], sub[c ^ 1], node[(c >> 1) ^ 1], child[(c >> 2) ^ 1]
        row = jnp.concatenate(
            [
                own[:, : 4 * unit],
                other[:, : 5 * unit],
                jnp.where(low, other[:, 5 * unit : 6 * unit], beside[:, 5 * unit : 6 * unit]),
                beside[:, 6 * unit : 9 * unit],
                across[:, 9 * unit :],
            ],
            axis=1,
        )
        out_ref[4 * c : 4 * c + 4] = jnp.broadcast_to(row[None], (4, 1, row.shape[1]))


def table(rows):
    return pl.pallas_call(
        table_kernel,
        in_specs=whole(1),
        out_specs=whole(1)[0],
        out_shape=jax.ShapeDtypeStruct((32, 1, rows.shape[2] // 11 * 15), F32),
        compiler_params=params(16),
        cost_estimate=cost(rows.size, 8 * rows.size),
        name="table",
    )(rows)


PAIRS = ((1, 0), (2, 0), (0, 0), (1, 1), (1, 2), (2, 2))


def gram_kernel(u_ref, keep_ref, send_ref, g_buf):
    rank = u_ref.shape[2]
    for place, (a, b) in enumerate(PAIRS):
        g_buf[:, place * rank : (place + 1) * rank] = dot(u_ref[a], u_ref[b], TN)
    half = rank // 2
    low = jnp.concatenate([g_buf[:half, : 3 * rank + half], g_buf[:half, 4 * rank :]], axis=1)
    high = jnp.concatenate([g_buf[half:, : 2 * rank], g_buf[half:, 2 * rank + half :]], axis=1)
    first_core = core_index() == 0
    keep_ref[...] = jnp.where(first_core, low, high)
    send_ref[...] = jnp.where(first_core, high, low)


def gram(bases):
    leaf, rank = bases.shape[1:]
    width = len(PAIRS) * rank
    shape = jax.ShapeDtypeStruct((rank // 2, width - rank // 2), F32)
    return pl.pallas_call(
        gram_kernel,
        in_specs=whole(1),
        out_specs=whole(2),
        out_shape=[shape, shape],
        scratch_shapes=[pltpu.VMEM((rank, width), F32)],
        compiler_params=params(24),
        cost_estimate=cost(12 * leaf * rank * rank, 6 * leaf * rank),
        name="gram",
    )(bases)


def first_kernel(b_ref, f_ref, u_ref, z_ref, keep_ref, send_ref, f_buf, u_buf, sems):
    leaf = f_ref.shape[0]
    rows = leaf // CHUNKS
    copies = [
        pltpu.make_async_copy(f_ref.at[pl.ds(i * rows, rows)], f_buf.at[pl.ds(i * rows, rows)], sems.at[i])
        for i in range(CHUNKS)
    ]
    copies.append(pltpu.make_async_copy(u_ref, u_buf, sems.at[CHUNKS]))
    for copy in copies:
        copy.start()
    b = b_ref[...]
    for i in range(CHUNKS):
        copies[i].wait()
        z_ref[:, i * rows : (i + 1) * rows] = dot(b, f_buf[i * rows : (i + 1) * rows], NT)
    copies[CHUNKS].wait()
    zb = z_ref[...].astype(BF16)
    split_halves(jnp.concatenate([dot(zb, u_buf[k]) for k in range(3)], axis=1), keep_ref, send_ref)


def first(rhs, inverse, bases):
    cols, leaf = rhs.shape
    rank = bases.shape[2]
    shape = jax.ShapeDtypeStruct((cols // 2, 3 * rank), F32)
    return pl.pallas_call(
        first_kernel,
        in_specs=whole(1) + whole(2, pltpu.HBM),
        out_specs=whole(3),
        out_shape=[jax.ShapeDtypeStruct((cols, leaf), F32), shape, shape],
        scratch_shapes=[
            pltpu.VMEM((leaf, leaf), BF16),
            pltpu.VMEM((3, leaf, rank), BF16),
            pltpu.SemaphoreType.DMA((CHUNKS + 1,)),
        ],
        compiler_params=params(61),
        cost_estimate=cost(2 * leaf * leaf * cols, 2 * leaf * leaf),
        name="first",
    )(rhs, inverse, bases)


def blocks(own_ref, other_ref):
    own, other = own_ref[...], other_ref[...]
    first_core = core_index() == 0
    low, high = jnp.where(first_core, own, other), jnp.where(first_core, other, own)
    unit = low.shape[1] // 15

    def at(half, k, count=1):
        return half[:, k * unit : (k + count) * unit]

    def square(left_top, right_top, left_bottom, right_bottom):
        top = jnp.concatenate([left_top, right_top], axis=1)
        return jnp.concatenate([top, jnp.concatenate([left_bottom, right_bottom], axis=1)], axis=0)

    m00 = square(at(low, 8), at(low, 9), at(low, 9).T, at(high, 8))
    m11 = square(at(low, 10), at(high, 9).T, at(high, 9), at(high, 10))
    plain = [jnp.concatenate([at(low, k, 2), at(high, k, 2)], axis=0) for k in (0, 2, 4, 6, 11, 13)]
    return plain[:4] + [m00, m11] + plain[4:]


def up_kernel(own_ref, other_ref, w_ref, both_ref, vs_ref, q_ref):
    m10, m20, m10o, m20o, m00o, _, m12o, _ = blocks(own_ref, other_ref)
    rank = m10.shape[0]
    p_ref, po_ref = both_ref[:, : 3 * rank], both_ref[:, 3 * rank :]
    q0 = exact(po_ref[:, :rank], w_ref[0], NT)
    q0o = exact(p_ref[:, :rank], w_ref[0], NT)
    s0o = po_ref[:, :rank] - apply(q0o, m00o, NN)
    s1 = p_ref[:, rank : 2 * rank] + po_ref[:, rank : 2 * rank] - apply(q0, m10, NT) - apply(q0o, m10o, NT)
    s2 = p_ref[:, 2 * rank :] + po_ref[:, 2 * rank :] - apply(q0, m20, NT) - apply(q0o, m20o, NT)
    q1o = exact(s1, w_ref[1], NT)
    vs_ref[...] = jnp.concatenate([s2 - apply(q1o, m12o, NN), s1], axis=1)
    q_ref[...] = jnp.concatenate([s0o, q0, q1o], axis=1)


def up(own, other, coupling, sums):
    rows, width = sums.shape[0], sums.shape[1] // 2
    rank = width // 3
    return pl.pallas_call(
        up_kernel,
        in_specs=whole(4),
        out_specs=whole(2),
        out_shape=[jax.ShapeDtypeStruct((rows, 2 * rank), F32), jax.ShapeDtypeStruct((rows, width), F32)],
        compiler_params=params(16),
        cost_estimate=cost(32 * rows * rank * rank, 8 * own.size),
        name="up",
    )(own, other, coupling, sums)


def down_kernel(own_ref, other_ref, w_ref, vs_ref, b_ref, r2_ref, r3_ref, q_ref, out_ref):
    m10o, m20o, _, m11o, m12o, m22o = blocks(own_ref, other_ref)[2:]
    rank = m10o.shape[0]
    s0o, q0, q1o = (q_ref[:, k * rank : (k + 1) * rank] for k in range(3))
    c2 = vs_ref[:, :rank] + b_ref[:, :rank]
    c2o = r2_ref[...] + r3_ref[...]
    s1o = b_ref[:, rank:]
    q1 = exact(s1o, w_ref[1], NT)
    q2 = exact(c2o, w_ref[2], NT)
    q2o = exact(c2, w_ref[2], NT)
    t2 = q2 + exact(c2o - apply(q2o, m22o, NN), w_ref[2], NN)
    t1 = q1 + exact(s1o - apply(q1o, m11o, NN) - apply(t2, m12o, NT), w_ref[1], NN)
    t0 = q0 + exact(s0o - apply(t1, m10o, NN) - apply(t2, m20o, NN), w_ref[0], NN)
    out_ref[...] = jnp.concatenate([t0, t1, t2], axis=1)


def down(own, other, coupling, vs, beside, r2, r3, q):
    rows, width = q.shape
    return pl.pallas_call(
        down_kernel,
        in_specs=whole(8),
        out_specs=whole(1)[0],
        out_shape=jax.ShapeDtypeStruct((rows, width), F32),
        compiler_params=params(16),
        cost_estimate=cost(4 * rows * width * width, 8 * own.size),
        name="down",
    )(own, other, coupling, vs, beside, r2, r3, q)


def last_kernel(own_ref, other_ref, u_ref, z_ref, f_ref, out_ref):
    leaf = f_ref.shape[0]
    rank = u_ref.shape[2]
    width = leaf // CHUNKS
    q = both(own_ref[...], other_ref[...]).astype(BF16)
    z = z_ref[...]
    for level in range(3):
        z -= dot(q[:, level * rank : (level + 1) * rank], u_ref[level], NT)
    zb = z.astype(BF16)
    for i in range(CHUNKS):
        at = slice(i * width, (i + 1) * width)
        out_ref[:, at] = dot(zb, f_ref[:, at]).astype(BF16)


def last(own, other, bases, state, inverse):
    cols, leaf = state.shape
    return pl.pallas_call(
        last_kernel,
        in_specs=whole(5),
        out_specs=whole(1)[0],
        out_shape=jax.ShapeDtypeStruct((cols, leaf), BF16),
        compiler_params=params(24),
        cost_estimate=cost(2 * leaf * leaf * cols, 2 * leaf * leaf),
        name="last",
    )(own, other, bases, state, inverse)


def stage_kernel(f_ref, u_ref, f_out, u_out, sems):
    rows = f_ref.shape[0] // 8
    copies = [
        pltpu.make_async_copy(f_ref.at[pl.ds(i * rows, rows)], f_out.at[pl.ds(i * rows, rows)], sems.at[i])
        for i in range(8)
    ]
    copies.append(pltpu.make_async_copy(u_ref, u_out, sems.at[8]))
    for copy in copies:
        copy.start()
    for copy in copies:
        copy.wait()


def stage(inverse, bases):
    return pl.pallas_call(
        stage_kernel,
        in_specs=whole(2, pltpu.HBM),
        out_specs=whole(2),
        out_shape=[pltpu.VMEM(inverse.shape, BF16), pltpu.VMEM(bases.shape, BF16)],
        scratch_shapes=[pltpu.SemaphoreType.DMA((9,))],
        compiler_params=params(48),
        cost_estimate=cost(0, 4 * inverse.size),
        name="stage",
    )(inverse, bases)


def after(value, *others):
    return lax.optimization_barrier((value, *others))[0]


def shards(rhs, leaf_inverse, bases, coupling):
    rank = bases.shape[2]

    keep, send = gram(bases)
    rows = split(keep, swap(send, 1))
    state, keep, send = first(after(rhs.T, *rows), leaf_inverse, bases)
    parts = split(keep, swap(send, 1))
    mine = add_rows([rows[0]] + [swap(rows[m], 2 * m) for m in (1, 2, 3)])
    summed = table(over_xz(after(mine, parts[0])))
    part = parts[0] + swap(parts[1], 2) + swap(parts[2], 4) + swap(parts[3], 6)
    pair = part + swap(part, 8)
    back = over_xz(after(summed, pair))
    p = pair + swap(pair, 16)
    po = swap(p, 56)

    mine = pack(back, p, po)
    own, half = unpack([mine] + [swap(mine, 2 * m) for m in (1, 2, 3)], p.shape[0], rank)
    sums = (own, swap(own, 1), coupling)

    vs, q = up(*sums, half)
    v = vs[:, :rank]
    inverse_v, bases_v = stage(*lax.optimization_barrier((leaf_inverse, bases, q))[:2])
    mine = down(*sums, vs, swap(vs, 64), swap(v, 128), swap(v, 192), after(q, inverse_v))
    return last(mine, swap(mine, 1), bases_v, state, inverse_v).T


def solution(mesh):
    placed = (P(AXIS, None), P(AXIS, None), P(None, AXIS, None), P())
    return jax.shard_map(
        shards, mesh=mesh, in_specs=placed, out_specs=P(AXIS, None), check_vma=False
    )
```

```python
import jax
import jax.numpy as jnp
from jax import lax
from jax.experimental import pallas as pl
from jax.experimental.pallas import tpu as pltpu
from jax.sharding import PartitionSpec as P

F32, BF16 = jnp.float32, jnp.bfloat16
AXIS = "leaf"
N = 256
VMEM = pltpu.VMEM
CHUNKS = 4


def params(mib):
    return pltpu.CompilerParams(vmem_limit_bytes=mib << 20)


def cost(flops, size):
    return pl.CostEstimate(flops=flops, bytes_accessed=size, transcendentals=0)


def whole(count, space=None):
    return [pl.BlockSpec(memory_space=space or VMEM)] * count


def dot(a, b, dims=((1,), (0,))):
    return lax.dot_general(a, b, (dims, ((), ())), preferred_element_type=F32)


NN, NT, TN = ((1,), (0,)), ((1,), (1,)), ((0,), (0,))


def swap(value, mask):
    return lax.ppermute(value, AXIS, [(i, i ^ mask) for i in range(N)])


def over_xz(value):
    groups = [[(x * 8 + z) * 8 + low for z in range(8) for x in range(4)] for low in range(8)]
    return lax.all_to_all(value, AXIS, 0, 0, axis_index_groups=groups, tiled=True)


def thrice(value):
    a = value.astype(BF16)
    rest = value - a.astype(F32)
    b = rest.astype(BF16)
    return jnp.concatenate([a, b, (rest - b.astype(F32)).astype(BF16)], axis=0)


def exact(value, weight, dims):
    rows = value.shape[0]
    out = dot(thrice(value), weight, dims)
    return out[:rows] + out[rows : 2 * rows] + out[2 * rows :]


def apply(value, matrix, dims):
    value, top = value.astype(BF16), matrix.astype(BF16)
    return dot(value, top, dims) + dot(value, (matrix - top.astype(F32)).astype(BF16), dims)


def core_index():
    return lax.axis_index(AXIS) & 1


def both(own, other):
    low = core_index() == 0
    return jnp.concatenate([jnp.where(low, own, other), jnp.where(low, other, own)], axis=0)


def split_halves(value, keep_ref, send_ref):
    half = value.shape[0] // 2
    low = core_index() == 0
    keep_ref[...] = jnp.where(low, value[:half], value[half:])
    send_ref[...] = jnp.where(low, value[half:], value[:half])


def split_kernel(keep_ref, other_ref, *outs):
    rows = outs[0].shape[0]
    y = (lax.axis_index(AXIS) >> 1) & 3
    for m, out in enumerate(outs):
        at = pl.ds(pl.multiple_of((y ^ m) * rows, rows), rows)
        out[...] = keep_ref[at, :] + other_ref[at, :]


def split(keep, other):
    shape = jax.ShapeDtypeStruct((keep.shape[0] // 4, keep.shape[1]), F32)
    return pl.pallas_call(
        split_kernel,
        in_specs=whole(2),
        out_specs=whole(4),
        out_shape=[shape] * 4,
        compiler_params=params(16),
        cost_estimate=cost(keep.size, 12 * keep.size),
        name="split",
    )(keep, other)


def pack_kernel(sums_ref, p_ref, po_ref, out_ref):
    rows, rank = sums_ref.shape[0], p_ref.shape[1] // 3
    out_ref[:rows] = sums_ref[...]
    for k in range(6):
        value = (p_ref if k < 3 else po_ref)[:, k % 3 * rank : (k % 3 + 1) * rank]
        for r in range(8):
            row, place = divmod(8 * k + r, 7)
            out_ref[rows + row, :, place * rank : (place + 1) * rank] = value[r : r + 1]


def pack(sums, p, po):
    rows, _, width = sums.shape
    return pl.pallas_call(
        pack_kernel,
        in_specs=whole(3),
        out_specs=whole(1)[0],
        out_shape=jax.ShapeDtypeStruct((rows + 7, 1, width), F32),
        compiler_params=params(16),
        cost_estimate=cost(0, 8 * rows * width),
        name="pack",
    )(sums, p, po)


def unpack_kernel(*refs):
    parts, own_ref, half_ref = refs[:4], refs[4], refs[5]
    rows, rank = own_ref.shape[0] // 4, half_ref.shape[1] // 6
    cols = half_ref.shape[0] // 4
    y = (lax.axis_index(AXIS) >> 1) & 3
    for m, part in enumerate(parts):
        at = pl.ds(pl.multiple_of((y ^ m) * rows, rows), rows)
        own_ref[at, :] = part[:rows].reshape(rows, own_ref.shape[1])
        at = pl.ds(pl.multiple_of((y ^ m) * cols, cols), cols)
        for k in range(6):
            places = [divmod(8 * k + r, 7) for r in range(8)]
            value = jnp.concatenate([part[rows + i, :, j * rank : (j + 1) * rank] for i, j in places], axis=0)
            half_ref[at, k * rank : (k + 1) * rank] = value


def unpack(parts, cols, rank):
    rows, width = parts[0].shape[0] - 7, parts[0].shape[2]
    return pl.pallas_call(
        unpack_kernel,
        in_specs=whole(4),
        out_specs=whole(2),
        out_shape=[jax.ShapeDtypeStruct((4 * rows, width), F32), jax.ShapeDtypeStruct((4 * cols, 6 * rank), F32)],
        compiler_params=params(16),
        cost_estimate=cost(0, 32 * rows * width),
        name="unpack",
    )(*parts)


def add_kernel(a, b, c, d, out):
    out[...] = (a[...] + b[...] + c[...] + d[...]).reshape(out.shape)


def add_rows(parts):
    rows, width = parts[0].shape
    return pl.pallas_call(
        add_kernel,
        in_specs=whole(4),
        out_specs=whole(1)[0],
        out_shape=jax.ShapeDtypeStruct((rows, 1, width), F32),
        compiler_params=params(16),
        cost_estimate=cost(rows * width, 12 * rows * width),
        name="add_rows",
    )(*parts)


def table_kernel(rows_ref, out_ref):
    unit = rows_ref.shape[2] // 11
    low = core_index() == 0
    sub = []
    for c in range(8):
        at = c % 2 * 16 + c // 2
        sub.append(rows_ref[at] + rows_ref[at + 4] + rows_ref[at + 8] + rows_ref[at + 12])
    node = [sub[2 * c] + sub[2 * c + 1] for c in range(4)]
    child = [node[0] + node[1], node[2] + node[3]]
    for c in range(8):
        own, other, beside, across = sub[c], sub[c ^ 1], node[(c >> 1) ^ 1], child[(c >> 2) ^ 1]
        row = jnp.concatenate(
            [
                own[:, : 4 * unit],
                other[:, : 5 * unit],
                jnp.where(low, other[:, 5 * unit : 6 * unit], beside[:, 5 * unit : 6 * unit]),
                beside[:, 6 * unit : 9 * unit],
                across[:, 9 * unit :],
            ],
            axis=1,
        )
        for k in range(4):
            out_ref[c % 2 * 16 + c // 2 + 4 * k] = row


def table(rows):
    return pl.pallas_call(
        table_kernel,
        in_specs=whole(1),
        out_specs=whole(1)[0],
        out_shape=jax.ShapeDtypeStruct((32, 1, rows.shape[2] // 11 * 15), F32),
        compiler_params=params(16),
        cost_estimate=cost(rows.size, 8 * rows.size),
        name="table",
    )(rows)


PAIRS = ((1, 0), (2, 0), (0, 0), (1, 1), (1, 2), (2, 2))


def gram_kernel(u_ref, keep_ref, send_ref, g_buf):
    rank = u_ref.shape[2]
    for place, (a, b) in enumerate(PAIRS):
        g_buf[:, place * rank : (place + 1) * rank] = dot(u_ref[a], u_ref[b], TN)
    half = rank // 2
    low = jnp.concatenate([g_buf[:half, : 3 * rank + half], g_buf[:half, 4 * rank :]], axis=1)
    high = jnp.concatenate([g_buf[half:, : 2 * rank], g_buf[half:, 2 * rank + half :]], axis=1)
    first_core = core_index() == 0
    keep_ref[...] = jnp.where(first_core, low, high)
    send_ref[...] = jnp.where(first_core, high, low)


def gram(bases):
    leaf, rank = bases.shape[1:]
    width = len(PAIRS) * rank
    shape = jax.ShapeDtypeStruct((rank // 2, width - rank // 2), F32)
    return pl.pallas_call(
        gram_kernel,
        in_specs=whole(1),
        out_specs=whole(2),
        out_shape=[shape, shape],
        scratch_shapes=[pltpu.VMEM((rank, width), F32)],
        compiler_params=params(24),
        cost_estimate=cost(12 * leaf * rank * rank, 6 * leaf * rank),
        name="gram",
    )(bases)


def first_kernel(b_ref, f_ref, u_ref, z_ref, keep_ref, send_ref, f_buf, u_buf, sems):
    leaf = f_ref.shape[0]
    rows = leaf // CHUNKS
    copies = [
        pltpu.make_async_copy(f_ref.at[pl.ds(i * rows, rows)], f_buf.at[pl.ds(i * rows, rows)], sems.at[i])
        for i in range(CHUNKS)
    ]
    copies.append(pltpu.make_async_copy(u_ref, u_buf, sems.at[CHUNKS]))
    for copy in copies:
        copy.start()
    b = b_ref[...]
    for i in range(CHUNKS):
        copies[i].wait()
        z_ref[:, i * rows : (i + 1) * rows] = dot(b, f_buf[i * rows : (i + 1) * rows], NT)
    copies[CHUNKS].wait()
    zb = z_ref[...].astype(BF16)
    split_halves(jnp.concatenate([dot(zb, u_buf[k]) for k in range(3)], axis=1), keep_ref, send_ref)


def first(rhs, inverse, bases):
    cols, leaf = rhs.shape
    rank = bases.shape[2]
    shape = jax.ShapeDtypeStruct((cols // 2, 3 * rank), F32)
    return pl.pallas_call(
        first_kernel,
        in_specs=whole(1) + whole(2, pltpu.HBM),
        out_specs=whole(3),
        out_shape=[jax.ShapeDtypeStruct((cols, leaf), F32), shape, shape],
        scratch_shapes=[
            pltpu.VMEM((leaf, leaf), BF16),
            pltpu.VMEM((3, leaf, rank), BF16),
            pltpu.SemaphoreType.DMA((CHUNKS + 1,)),
        ],
        compiler_params=params(61),
        cost_estimate=cost(2 * leaf * leaf * cols, 2 * leaf * leaf),
        name="first",
    )(rhs, inverse, bases)


def blocks(own_ref, other_ref):
    own, other = own_ref[...], other_ref[...]
    first_core = core_index() == 0
    low, high = jnp.where(first_core, own, other), jnp.where(first_core, other, own)
    unit = low.shape[1] // 15

    def at(half, k, count=1):
        return half[:, k * unit : (k + count) * unit]

    def square(left_top, right_top, left_bottom, right_bottom):
        top = jnp.concatenate([left_top, right_top], axis=1)
        return jnp.concatenate([top, jnp.concatenate([left_bottom, right_bottom], axis=1)], axis=0)

    m00 = square(at(low, 8), at(low, 9), at(low, 9).T, at(high, 8))
    m11 = square(at(low, 10), at(high, 9).T, at(high, 9), at(high, 10))
    plain = [jnp.concatenate([at(low, k, 2), at(high, k, 2)], axis=0) for k in (0, 2, 4, 6, 11, 13)]
    return plain[:4] + [m00, m11] + plain[4:]


def up_kernel(own_ref, other_ref, w_ref, both_ref, vs_ref, q_ref):
    m10, m20, m10o, m20o, m00o, _, m12o, _ = blocks(own_ref, other_ref)
    rank = m10.shape[0]
    p_ref, po_ref = both_ref[:, : 3 * rank], both_ref[:, 3 * rank :]
    q0 = exact(po_ref[:, :rank], w_ref[0], NT)
    q0o = exact(p_ref[:, :rank], w_ref[0], NT)
    s0o = po_ref[:, :rank] - apply(q0o, m00o, NN)
    s1 = p_ref[:, rank : 2 * rank] + po_ref[:, rank : 2 * rank] - apply(q0, m10, NT) - apply(q0o, m10o, NT)
    s2 = p_ref[:, 2 * rank :] + po_ref[:, 2 * rank :] - apply(q0, m20, NT) - apply(q0o, m20o, NT)
    q1o = exact(s1, w_ref[1], NT)
    vs_ref[...] = jnp.concatenate([s2 - apply(q1o, m12o, NN), s1], axis=1)
    q_ref[...] = jnp.concatenate([s0o, q0, q1o], axis=1)


def up(own, other, coupling, sums):
    rows, width = sums.shape[0], sums.shape[1] // 2
    rank = width // 3
    return pl.pallas_call(
        up_kernel,
        in_specs=whole(4),
        out_specs=whole(2),
        out_shape=[jax.ShapeDtypeStruct((rows, 2 * rank), F32), jax.ShapeDtypeStruct((rows, width), F32)],
        compiler_params=params(16),
        cost_estimate=cost(32 * rows * rank * rank, 8 * own.size),
        name="up",
    )(own, other, coupling, sums)


def down_kernel(own_ref, other_ref, w_ref, vs_ref, b_ref, r2_ref, r3_ref, q_ref, out_ref):
    m10o, m20o, _, m11o, m12o, m22o = blocks(own_ref, other_ref)[2:]
    rank = m10o.shape[0]
    s0o, q0, q1o = (q_ref[:, k * rank : (k + 1) * rank] for k in range(3))
    c2 = vs_ref[:, :rank] + b_ref[:, :rank]
    c2o = r2_ref[...] + r3_ref[...]
    s1o = b_ref[:, rank:]
    q1 = exact(s1o, w_ref[1], NT)
    q2 = exact(c2o, w_ref[2], NT)
    q2o = exact(c2, w_ref[2], NT)
    t2 = q2 + exact(c2o - apply(q2o, m22o, NN), w_ref[2], NN)
    t1 = q1 + exact(s1o - apply(q1o, m11o, NN) - apply(t2, m12o, NT), w_ref[1], NN)
    t0 = q0 + exact(s0o - apply(t1, m10o, NN) - apply(t2, m20o, NN), w_ref[0], NN)
    out_ref[...] = jnp.concatenate([t0, t1, t2], axis=1)


def down(own, other, coupling, vs, beside, r2, r3, q):
    rows, width = q.shape
    return pl.pallas_call(
        down_kernel,
        in_specs=whole(8),
        out_specs=whole(1)[0],
        out_shape=jax.ShapeDtypeStruct((rows, width), F32),
        compiler_params=params(16),
        cost_estimate=cost(4 * rows * width * width, 8 * own.size),
        name="down",
    )(own, other, coupling, vs, beside, r2, r3, q)


def last_kernel(own_ref, other_ref, u_ref, z_ref, f_ref, out_ref):
    leaf = f_ref.shape[0]
    rank = u_ref.shape[2]
    width = leaf // CHUNKS
    q = both(own_ref[...], other_ref[...]).astype(BF16)
    z = z_ref[...]
    for level in range(3):
        z -= dot(q[:, level * rank : (level + 1) * rank], u_ref[level], NT)
    zb = z.astype(BF16)
    for i in range(CHUNKS):
        at = slice(i * width, (i + 1) * width)
        out_ref[:, at] = dot(zb, f_ref[:, at]).astype(BF16)


def last(own, other, bases, state, inverse):
    cols, leaf = state.shape
    return pl.pallas_call(
        last_kernel,
        in_specs=whole(5),
        out_specs=whole(1)[0],
        out_shape=jax.ShapeDtypeStruct((cols, leaf), BF16),
        compiler_params=params(24),
        cost_estimate=cost(2 * leaf * leaf * cols, 2 * leaf * leaf),
        name="last",
    )(own, other, bases, state, inverse)


def stage_kernel(f_ref, u_ref, f_out, u_out, sems):
    rows = f_ref.shape[0] // 8
    copies = [
        pltpu.make_async_copy(f_ref.at[pl.ds(i * rows, rows)], f_out.at[pl.ds(i * rows, rows)], sems.at[i])
        for i in range(8)
    ]
    copies.append(pltpu.make_async_copy(u_ref, u_out, sems.at[8]))
    for copy in copies:
        copy.start()
    for copy in copies:
        copy.wait()


def stage(inverse, bases):
    return pl.pallas_call(
        stage_kernel,
        in_specs=whole(2, pltpu.HBM),
        out_specs=whole(2),
        out_shape=[pltpu.VMEM(inverse.shape, BF16), pltpu.VMEM(bases.shape, BF16)],
        scratch_shapes=[pltpu.SemaphoreType.DMA((9,))],
        compiler_params=params(48),
        cost_estimate=cost(0, 4 * inverse.size),
        name="stage",
    )(inverse, bases)


def after(value, *others):
    return lax.optimization_barrier((value, *others))[0]


def shards(rhs, leaf_inverse, bases, coupling):
    rank = bases.shape[2]

    keep, send = gram(bases)
    rows = split(keep, swap(send, 1))
    state, keep, send = first(after(rhs.T, *rows), leaf_inverse, bases)
    parts = split(keep, swap(send, 1))
    mine = add_rows([rows[0]] + [swap(rows[m], 2 * m) for m in (1, 2, 3)])
    summed = table(over_xz(after(mine, send)))
    part = parts[0] + swap(parts[1], 2) + swap(parts[2], 4) + swap(parts[3], 6)
    pair = part + swap(part, 8)
    back = over_xz(after(summed, part))
    p = pair + swap(pair, 16)
    po = swap(p, 56)

    mine = pack(back, p, po)
    own, half = unpack([mine] + [swap(mine, 2 * m) for m in (1, 2, 3)], p.shape[0], rank)
    sums = (own, swap(own, 1), coupling)

    vs, q = up(*sums, half)
    v = vs[:, :rank]
    inverse_v, bases_v = stage(*lax.optimization_barrier((leaf_inverse, bases, q))[:2])
    mine = down(*sums, vs, swap(vs, 64), swap(v, 128), swap(v, 192), after(q, inverse_v))
    return last(mine, swap(mine, 1), bases_v, state, inverse_v).T


def solution(mesh):
    placed = (P(AXIS, None), P(AXIS, None), P(None, AXIS, None), P())
    return jax.shard_map(
        shards, mesh=mesh, in_specs=placed, out_specs=P(AXIS, None), check_vma=False
    )
```

```python
import jax
import jax.numpy as jnp
from jax import lax
from jax.experimental import pallas as pl
from jax.experimental.pallas import tpu as pltpu
from jax.sharding import PartitionSpec as P

F32, BF16 = jnp.float32, jnp.bfloat16
AXIS = "leaf"
N = 256
VMEM = pltpu.VMEM
CHUNKS = 4


def params(mib):
    return pltpu.CompilerParams(vmem_limit_bytes=mib << 20)


def cost(flops, size):
    return pl.CostEstimate(flops=flops, bytes_accessed=size, transcendentals=0)


def whole(count, space=None):
    return [pl.BlockSpec(memory_space=space or VMEM)] * count


def dot(a, b, dims=((1,), (0,))):
    return lax.dot_general(a, b, (dims, ((), ())), preferred_element_type=F32)


NN, NT, TN = ((1,), (0,)), ((1,), (1,)), ((0,), (0,))


def swap(value, mask):
    return lax.ppermute(value, AXIS, [(i, i ^ mask) for i in range(N)])


def over_xz(value):
    groups = [[(x * 8 + z) * 8 + low for z in range(8) for x in range(4)] for low in range(8)]
    return lax.all_to_all(value, AXIS, 0, 0, axis_index_groups=groups, tiled=True)


def thrice(value):
    a = value.astype(BF16)
    rest = value - a.astype(F32)
    b = rest.astype(BF16)
    return jnp.concatenate([a, b, (rest - b.astype(F32)).astype(BF16)], axis=0)


def exact(value, weight, dims):
    rows = value.shape[0]
    out = dot(thrice(value), weight, dims)
    return out[:rows] + out[rows : 2 * rows] + out[2 * rows :]


def apply(value, matrix, dims):
    value, top = value.astype(BF16), matrix.astype(BF16)
    return dot(value, top, dims) + dot(value, (matrix - top.astype(F32)).astype(BF16), dims)


def core_index():
    return lax.axis_index(AXIS) & 1


def both(own, other):
    low = core_index() == 0
    return jnp.concatenate([jnp.where(low, own, other), jnp.where(low, other, own)], axis=0)


def split_halves(value, keep_ref, send_ref):
    half = value.shape[0] // 2
    low = core_index() == 0
    keep_ref[...] = jnp.where(low, value[:half], value[half:])
    send_ref[...] = jnp.where(low, value[half:], value[:half])


def split_kernel(keep_ref, other_ref, *outs):
    rows = outs[0].shape[0]
    y = (lax.axis_index(AXIS) >> 1) & 3
    for m, out in enumerate(outs):
        at = pl.ds(pl.multiple_of((y ^ m) * rows, rows), rows)
        out[...] = keep_ref[at, :] + other_ref[at, :]


def split(keep, other):
    shape = jax.ShapeDtypeStruct((keep.shape[0] // 4, keep.shape[1]), F32)
    return pl.pallas_call(
        split_kernel,
        in_specs=whole(2),
        out_specs=whole(4),
        out_shape=[shape] * 4,
        compiler_params=params(16),
        cost_estimate=cost(keep.size, 12 * keep.size),
        name="split",
    )(keep, other)


def pack_kernel(sums_ref, p_ref, po_ref, out_ref):
    rows, rank = sums_ref.shape[0], p_ref.shape[1] // 3
    out_ref[:rows] = sums_ref[...]
    for k in range(6):
        value = (p_ref if k < 3 else po_ref)[:, k % 3 * rank : (k % 3 + 1) * rank]
        for r in range(8):
            row, place = divmod(8 * k + r, 7)
            out_ref[rows + row, :, place * rank : (place + 1) * rank] = value[r : r + 1]


def pack(sums, p, po):
    rows, _, width = sums.shape
    return pl.pallas_call(
        pack_kernel,
        in_specs=whole(3),
        out_specs=whole(1)[0],
        out_shape=jax.ShapeDtypeStruct((rows + 7, 1, width), F32),
        compiler_params=params(16),
        cost_estimate=cost(0, 8 * rows * width),
        name="pack",
    )(sums, p, po)


def unpack_kernel(*refs):
    parts, own_ref, half_ref = refs[:4], refs[4], refs[5]
    rows, rank = own_ref.shape[0] // 4, half_ref.shape[1] // 6
    cols = half_ref.shape[0] // 4
    y = (lax.axis_index(AXIS) >> 1) & 3
    for m, part in enumerate(parts):
        at = pl.ds(pl.multiple_of((y ^ m) * rows, rows), rows)
        own_ref[at, :] = part[:rows].reshape(rows, own_ref.shape[1])
        at = pl.ds(pl.multiple_of((y ^ m) * cols, cols), cols)
        for k in range(6):
            places = [divmod(8 * k + r, 7) for r in range(8)]
            value = jnp.concatenate([part[rows + i, :, j * rank : (j + 1) * rank] for i, j in places], axis=0)
            half_ref[at, k * rank : (k + 1) * rank] = value


def unpack(parts, cols, rank):
    rows, width = parts[0].shape[0] - 7, parts[0].shape[2]
    return pl.pallas_call(
        unpack_kernel,
        in_specs=whole(4),
        out_specs=whole(2),
        out_shape=[jax.ShapeDtypeStruct((4 * rows, width), F32), jax.ShapeDtypeStruct((4 * cols, 6 * rank), F32)],
        compiler_params=params(16),
        cost_estimate=cost(0, 32 * rows * width),
        name="unpack",
    )(*parts)


def add_kernel(a, b, c, d, out):
    out[...] = (a[...] + b[...] + c[...] + d[...]).reshape(out.shape)


def add_rows(parts):
    rows, width = parts[0].shape
    return pl.pallas_call(
        add_kernel,
        in_specs=whole(4),
        out_specs=whole(1)[0],
        out_shape=jax.ShapeDtypeStruct((rows, 1, width), F32),
        compiler_params=params(16),
        cost_estimate=cost(rows * width, 12 * rows * width),
        name="add_rows",
    )(*parts)


def table_kernel(rows_ref, out_ref):
    unit = rows_ref.shape[2] // 11
    low = core_index() == 0
    sub = []
    for c in range(8):
        at = c % 2 * 16 + c // 2
        sub.append(rows_ref[at] + rows_ref[at + 4] + rows_ref[at + 8] + rows_ref[at + 12])
    node = [sub[2 * c] + sub[2 * c + 1] for c in range(4)]
    child = [node[0] + node[1], node[2] + node[3]]
    for c in range(8):
        own, other, beside, across = sub[c], sub[c ^ 1], node[(c >> 1) ^ 1], child[(c >> 2) ^ 1]
        row = jnp.concatenate(
            [
                own[:, : 4 * unit],
                other[:, : 5 * unit],
                jnp.where(low, other[:, 5 * unit : 6 * unit], beside[:, 5 * unit : 6 * unit]),
                beside[:, 6 * unit : 9 * unit],
                across[:, 9 * unit :],
            ],
            axis=1,
        )
        for k in range(4):
            out_ref[c % 2 * 16 + c // 2 + 4 * k] = row


def table(rows):
    return pl.pallas_call(
        table_kernel,
        in_specs=whole(1),
        out_specs=whole(1)[0],
        out_shape=jax.ShapeDtypeStruct((32, 1, rows.shape[2] // 11 * 15), F32),
        compiler_params=params(16),
        cost_estimate=cost(rows.size, 8 * rows.size),
        name="table",
    )(rows)


PAIRS = ((1, 0), (2, 0), (0, 0), (1, 1), (1, 2), (2, 2))


def gram_kernel(u_ref, keep_ref, send_ref, g_buf):
    rank = u_ref.shape[2]
    for place, (a, b) in enumerate(PAIRS):
        g_buf[:, place * rank : (place + 1) * rank] = dot(u_ref[a], u_ref[b], TN)
    half = rank // 2
    low = jnp.concatenate([g_buf[:half, : 3 * rank + half], g_buf[:half, 4 * rank :]], axis=1)
    high = jnp.concatenate([g_buf[half:, : 2 * rank], g_buf[half:, 2 * rank + half :]], axis=1)
    first_core = core_index() == 0
    keep_ref[...] = jnp.where(first_core, low, high)
    send_ref[...] = jnp.where(first_core, high, low)


def gram(bases):
    leaf, rank = bases.shape[1:]
    width = len(PAIRS) * rank
    shape = jax.ShapeDtypeStruct((rank // 2, width - rank // 2), F32)
    return pl.pallas_call(
        gram_kernel,
        in_specs=whole(1),
        out_specs=whole(2),
        out_shape=[shape, shape],
        scratch_shapes=[pltpu.VMEM((rank, width), F32)],
        compiler_params=params(24),
        cost_estimate=cost(12 * leaf * rank * rank, 6 * leaf * rank),
        name="gram",
    )(bases)


def first_kernel(b_ref, f_ref, u_ref, z_ref, keep_ref, send_ref, f_buf, u_buf, sems):
    leaf = f_ref.shape[0]
    rows = leaf // CHUNKS
    copies = [
        pltpu.make_async_copy(f_ref.at[pl.ds(i * rows, rows)], f_buf.at[pl.ds(i * rows, rows)], sems.at[i])
        for i in range(CHUNKS)
    ]
    copies.append(pltpu.make_async_copy(u_ref, u_buf, sems.at[CHUNKS]))
    for copy in copies:
        copy.start()
    b = b_ref[...]
    for i in range(CHUNKS):
        copies[i].wait()
        z_ref[:, i * rows : (i + 1) * rows] = dot(b, f_buf[i * rows : (i + 1) * rows], NT)
    copies[CHUNKS].wait()
    zb = z_ref[...].astype(BF16)
    split_halves(jnp.concatenate([dot(zb, u_buf[k]) for k in range(3)], axis=1), keep_ref, send_ref)


def first(rhs, inverse, bases):
    cols, leaf = rhs.shape
    rank = bases.shape[2]
    shape = jax.ShapeDtypeStruct((cols // 2, 3 * rank), F32)
    return pl.pallas_call(
        first_kernel,
        in_specs=whole(1) + whole(2, pltpu.HBM),
        out_specs=whole(3),
        out_shape=[jax.ShapeDtypeStruct((cols, leaf), F32), shape, shape],
        scratch_shapes=[
            pltpu.VMEM((leaf, leaf), BF16),
            pltpu.VMEM((3, leaf, rank), BF16),
            pltpu.SemaphoreType.DMA((CHUNKS + 1,)),
        ],
        compiler_params=params(61),
        cost_estimate=cost(2 * leaf * leaf * cols, 2 * leaf * leaf),
        name="first",
    )(rhs, inverse, bases)


def blocks(own_ref, other_ref):
    own, other = own_ref[...], other_ref[...]
    first_core = core_index() == 0
    low, high = jnp.where(first_core, own, other), jnp.where(first_core, other, own)
    unit = low.shape[1] // 15

    def at(half, k, count=1):
        return half[:, k * unit : (k + count) * unit]

    def square(left_top, right_top, left_bottom, right_bottom):
        top = jnp.concatenate([left_top, right_top], axis=1)
        return jnp.concatenate([top, jnp.concatenate([left_bottom, right_bottom], axis=1)], axis=0)

    m00 = square(at(low, 8), at(low, 9), at(low, 9).T, at(high, 8))
    m11 = square(at(low, 10), at(high, 9).T, at(high, 9), at(high, 10))
    plain = [jnp.concatenate([at(low, k, 2), at(high, k, 2)], axis=0) for k in (0, 2, 4, 6, 11, 13)]
    return plain[:4] + [m00, m11] + plain[4:]


def up_kernel(own_ref, other_ref, w_ref, both_ref, vs_ref, q_ref):
    m10, m20, m10o, m20o, m00o, _, m12o, _ = blocks(own_ref, other_ref)
    rank = m10.shape[0]
    p_ref, po_ref = both_ref[:, : 3 * rank], both_ref[:, 3 * rank :]
    q0 = exact(po_ref[:, :rank], w_ref[0], NT)
    q0o = exact(p_ref[:, :rank], w_ref[0], NT)
    s0o = po_ref[:, :rank] - apply(q0o, m00o, NN)
    s1 = p_ref[:, rank : 2 * rank] + po_ref[:, rank : 2 * rank] - apply(q0, m10, NT) - apply(q0o, m10o, NT)
    s2 = p_ref[:, 2 * rank :] + po_ref[:, 2 * rank :] - apply(q0, m20, NT) - apply(q0o, m20o, NT)
    q1o = exact(s1, w_ref[1], NT)
    vs_ref[...] = jnp.concatenate([s2 - apply(q1o, m12o, NN), s1], axis=1)
    q_ref[...] = jnp.concatenate([s0o, q0, q1o], axis=1)


def up(own, other, coupling, sums):
    rows, width = sums.shape[0], sums.shape[1] // 2
    rank = width // 3
    return pl.pallas_call(
        up_kernel,
        in_specs=whole(4),
        out_specs=whole(2),
        out_shape=[jax.ShapeDtypeStruct((rows, 2 * rank), F32), jax.ShapeDtypeStruct((rows, width), F32)],
        compiler_params=params(16),
        cost_estimate=cost(32 * rows * rank * rank, 8 * own.size),
        name="up",
    )(own, other, coupling, sums)


def down_kernel(own_ref, other_ref, w_ref, vs_ref, b_ref, r2_ref, r3_ref, q_ref, out_ref):
    m10o, m20o, _, m11o, m12o, m22o = blocks(own_ref, other_ref)[2:]
    rank = m10o.shape[0]
    s0o, q0, q1o = (q_ref[:, k * rank : (k + 1) * rank] for k in range(3))
    c2 = vs_ref[:, :rank] + b_ref[:, :rank]
    c2o = r2_ref[...] + r3_ref[...]
    s1o = b_ref[:, rank:]
    q1 = exact(s1o, w_ref[1], NT)
    q2 = exact(c2o, w_ref[2], NT)
    q2o = exact(c2, w_ref[2], NT)
    t2 = q2 + exact(c2o - apply(q2o, m22o, NN), w_ref[2], NN)
    t1 = q1 + exact(s1o - apply(q1o, m11o, NN) - apply(t2, m12o, NT), w_ref[1], NN)
    t0 = q0 + exact(s0o - apply(t1, m10o, NN) - apply(t2, m20o, NN), w_ref[0], NN)
    out_ref[...] = jnp.concatenate([t0, t1, t2], axis=1)


def down(own, other, coupling, vs, beside, r2, r3, q):
    rows, width = q.shape
    return pl.pallas_call(
        down_kernel,
        in_specs=whole(8),
        out_specs=whole(1)[0],
        out_shape=jax.ShapeDtypeStruct((rows, width), F32),
        compiler_params=params(16),
        cost_estimate=cost(4 * rows * width * width, 8 * own.size),
        name="down",
    )(own, other, coupling, vs, beside, r2, r3, q)


def last_kernel(own_ref, other_ref, u_ref, z_ref, f_ref, out_ref):
    leaf = f_ref.shape[0]
    rank = u_ref.shape[2]
    width = leaf // CHUNKS
    q = both(own_ref[...], other_ref[...]).astype(BF16)
    z = z_ref[...]
    for level in range(3):
        z -= dot(q[:, level * rank : (level + 1) * rank], u_ref[level], NT)
    zb = z.astype(BF16)
    for i in range(CHUNKS):
        at = slice(i * width, (i + 1) * width)
        out_ref[:, at] = dot(zb, f_ref[:, at]).astype(BF16)


def last(own, other, bases, state, inverse):
    cols, leaf = state.shape
    return pl.pallas_call(
        last_kernel,
        in_specs=whole(5),
        out_specs=whole(1)[0],
        out_shape=jax.ShapeDtypeStruct((cols, leaf), BF16),
        compiler_params=params(24),
        cost_estimate=cost(2 * leaf * leaf * cols, 2 * leaf * leaf),
        name="last",
    )(own, other, bases, state, inverse)


def stage_kernel(f_ref, u_ref, f_out, u_out, sems):
    rows = f_ref.shape[0] // 8
    copies = [
        pltpu.make_async_copy(f_ref.at[pl.ds(i * rows, rows)], f_out.at[pl.ds(i * rows, rows)], sems.at[i])
        for i in range(8)
    ]
    copies.append(pltpu.make_async_copy(u_ref, u_out, sems.at[8]))
    for copy in copies:
        copy.start()
    for copy in copies:
        copy.wait()


def stage(inverse, bases):
    return pl.pallas_call(
        stage_kernel,
        in_specs=whole(2, pltpu.HBM),
        out_specs=whole(2),
        out_shape=[pltpu.VMEM(inverse.shape, BF16), pltpu.VMEM(bases.shape, BF16)],
        scratch_shapes=[pltpu.SemaphoreType.DMA((9,))],
        compiler_params=params(48),
        cost_estimate=cost(0, 4 * inverse.size),
        name="stage",
    )(inverse, bases)


def after(value, *others):
    return lax.optimization_barrier((value, *others))[0]


def shards(rhs, leaf_inverse, bases, coupling):
    rank = bases.shape[2]

    keep, send = gram(bases)
    rows = split(keep, swap(send, 1))
    state, keep, send = first(after(rhs.T, *rows), leaf_inverse, bases)
    parts = split(keep, swap(send, 1))
    mine = add_rows([rows[0]] + [swap(rows[m], 2 * m) for m in (2, 1, 3)])
    summed = table(over_xz(after(mine, send)))
    part = parts[0] + swap(parts[1], 2) + swap(parts[2], 4) + swap(parts[3], 6)
    pair = part + swap(part, 8)
    back = over_xz(after(summed, part))
    p = pair + swap(pair, 16)
    po = swap(p, 56)

    mine = pack(back, p, po)
    own, half = unpack([mine] + [swap(mine, 2 * m) for m in (1, 2, 3)], p.shape[0], rank)
    sums = (own, swap(own, 1), coupling)

    vs, q = up(*sums, half)
    v = vs[:, :rank]
    inverse_v, bases_v = stage(*lax.optimization_barrier((leaf_inverse, bases, q))[:2])
    mine = down(*sums, vs, swap(vs, 64), swap(v, 128), swap(v, 192), after(q, inverse_v))
    return last(mine, swap(mine, 1), bases_v, state, inverse_v).T


def solution(mesh):
    placed = (P(AXIS, None), P(AXIS, None), P(None, AXIS, None), P())
    return jax.shard_map(
        shards, mesh=mesh, in_specs=placed, out_specs=P(AXIS, None), check_vma=False
    )
```
